128 devices in a mesh: rows: 16 (over z, y), cols: 8 (over x, core).
Axes of the slice: x: 4, y: 4, z: 4, core: 2. Of those that a mesh axis runs over, the one named last changes fastest.
Arguments:
- history: bfloat16 [384, 128, 1024], P(('rows', 'cols')), may hold values from -24 to 24
- qkv_weight: bfloat16 [1024, 3072], replicated, may hold values from -0.1875 to 0.1875
- out_weight: bfloat16 [1024, 1024], replicated, may hold values from -0.1875 to 0.1875
- pool_weight: bfloat16 [1024, 1024], replicated, may hold values from -0.1875 to 0.1875
- head_weight: bfloat16 [1024, 1024], replicated, may hold values from -0.1875 to 0.1875
- risk_weight: float32 [1024], replicated, may hold values from -0.1875 to 0.1875
- time_table: float32 [128, 1024], replicated, may hold values from -3 to 3
- case_rows: int32 [384], P(('rows', 'cols')), may hold values from 0 to 2, as said below
- control_rows: int32 [384, 32], P(('rows', 'cols')), may hold values from 0 to 383, as said below
- buckets: int32 [384], P(('rows', 'cols')), may hold values from 0 to 127
- case_weight: float32 [384], P(('rows', 'cols')), may hold values from 8 to 64
Outputs:
- grad_input: float32 [384, 128, 1024], P(('rows', 'cols'))
- grad_qkv: float32 [1024, 3072], P(('rows', 'cols'))
- grad_out: float32 [1024, 1024], P(('rows', 'cols'))
- grad_pool: float32 [1024, 1024], P(('rows', 'cols'))
- grad_head: float32 [1024, 1024], P(('rows', 'cols'))
The draws below stay inside these ranges and needn't reach their ends.
Inputs may be any that keep to these rules, and one draw needn't show every extreme that they name: `case_rows`: the 3 cases of one device name distinct histories of that device, counted from 0. `control_rows`: history r lies on the device at place r // 3 along rows+cols. Among the controls of one device's cases, at most 4 lie on any one device, and for every device's cases some device holds exactly 4 of them.
All inputs are finite; a program needn't handle non-finite values.
Results may differ from the reference program's by a relative error of at most 0.015.
Values may be sent and summed in bfloat16 or wider, within the bound.
A program may use at most 128 MiB of HBM per device.

```python
import math
import jax
import jax.numpy as jnp
from jax import lax

D = 1024
HD = 64
HEADS = 16
DH = 1024
S = 128
K = 32
CAP = 4
NB = 128
R_DEV = 3
C_DEV = 3
ROWS = 384
CASES = 384
N_ROWS = 16
N_COLS = 8


def draw_case_rows(key, part):
    key = jax.random.fold_in(key, 3)
    devices = N_ROWS * N_COLS
    device_keys = jax.random.split(key, devices)

    def one_device(device_key):
        return jax.random.permutation(device_key, R_DEV)[:C_DEV].astype(jnp.int32)
    return jax.vmap(one_device)(device_keys).reshape(C_DEV * devices)


def draw_control_rows(key, part):
    key = jax.random.fold_in(key, 7)
    devices = N_ROWS * N_COLS
    pairs = C_DEV * K
    total_slots = devices * CAP
    hot_key, slot_key = jax.random.split(key)
    hot_owners = jax.random.permutation(hot_key, devices)[:4]
    slot_owner = jnp.arange(total_slots, dtype=jnp.int32) // CAP
    is_hot = jnp.any(slot_owner[:, None] == hot_owners[None, :], axis=1).astype(jnp.int32)

    def one_device(device_key):
        noise_key, order_key, row_key = jax.random.split(device_key, 3)
        noise_draw = jax.random.randint(noise_key, (total_slots,), 0, 1024)
        ranking = (noise_draw + 1024 * is_hot) * total_slots + jnp.arange(total_slots, dtype=jnp.int32)
        unused, chosen = lax.top_k(ranking, pairs)
        owners = jax.random.permutation(order_key, chosen // CAP)
        local_row = jax.random.randint(row_key, (pairs,), 0, R_DEV)
        return (owners * R_DEV + local_row).astype(jnp.int32).reshape(C_DEV, K)
    device_keys = jax.random.split(slot_key, devices)
    return jax.vmap(one_device)(device_keys).reshape(C_DEV * devices, K)


def place_ends(result, key, smallest, largest):
    spot = [jax.random.randint(jax.random.fold_in(key, axis), (), 0, length) for axis, length in enumerate(result.shape)]
    longest = result.shape.index(max(result.shape))
    beside = spot[:longest] + [(spot[longest] + 1) % result.shape[longest]] + spot[longest + 1:]
    return result.at[tuple(spot)].set(smallest).at[tuple(beside)].set(largest)


def spiked(values, own_key, source, target, blocks, factor):
    owner, partner = [(jnp.arange(values.shape[dim]) // (values.shape[dim] // blocks)).reshape([-1 if axis == dim else 1 for axis in range(values.ndim)]) for dim in (source, target)]
    chosen = jax.random.permutation(own_key, blocks)[partner]
    strong = (owner == chosen) | (owner == (partner + blocks // 2) % blocks)
    return jnp.where(strong, factor * values, values)


def shard_levels(rng, extent, shards, least, high):
    def one(dim, blocks):
        draws = jax.random.uniform(jax.random.fold_in(jax.random.fold_in(rng, 6), dim), (blocks,), jnp.float32, least / len(shards), high / len(shards))
        return jnp.repeat(jnp.exp(draws), extent[dim] // blocks).reshape((-1,) + (1,) * (len(extent) - dim - 1))

    loudness = one(*shards[0])
    for cut in shards[1:]:
        loudness = loudness * one(*cut)
    return loudness


def scatter_about(rng, dims, width, most, pieces=(), kind=jnp.bfloat16):
    entries = jax.random.normal(rng, dims, jnp.float32) * width
    if len(pieces) > 0:
        entries = shard_levels(rng, dims, pieces, -0.22, 0.18) * entries
    return jnp.clip(entries, min=-most, max=most).astype(kind)


def heavy_noise(stream_key, extent, scale, most, pieces, heavy, kind=jnp.bfloat16):
    array = scale * jax.random.normal(stream_key, extent, jnp.float32)
    if pieces:
        array = array * shard_levels(stream_key, extent, pieces, -0.22, 0.18)
    return jnp.clip(spiked(array, jax.random.fold_in(stream_key, 3), *heavy), -most, most).astype(kind)


def setup_inputs(seed: int = 0) -> dict:
    splits = jax.random.split(jax.random.key(seed), 12)
    return {
        "history": heavy_noise(splits[0], (ROWS, S, D), 1.0, 24.0, ((0, 128),), (0, 2, 128, 5.5)),
        "qkv_weight": scatter_about(splits[1], (D, 3 * D), D ** -0.5, 0.1875),
        "out_weight": scatter_about(splits[2], (D, D), D ** -0.5, 0.1875),
        "pool_weight": scatter_about(splits[3], (D, D), D ** -0.5, 0.1875),
        "head_weight": scatter_about(splits[4], (D, DH), D ** -0.5, 0.1875),
        "risk_weight": scatter_about(splits[5], (DH,), DH ** -0.5, 0.1875, (), jnp.float32),
        "time_table": scatter_about(splits[6], (NB, D), 0.5, 3.0, (), jnp.float32),
        "case_rows": draw_case_rows(jax.random.fold_in(splits[11], 71), 0),
        "control_rows": draw_control_rows(jax.random.fold_in(splits[11], 71), 0),
        "buckets": place_ends(jax.random.randint(splits[9], (CASES,), 0, NB), jax.random.fold_in(splits[9], 1), 0, NB - 1).astype(jnp.int32),
        "case_weight": jnp.clip(jnp.exp(math.log(64.0) - 2.0794415 * jax.random.uniform(splits[10], (CASES,), jnp.float32) ** shard_levels(splits[10], (CASES,), ((0, 128),), -0.2, 0.2)), 8.0, 64.0),
    }


def to_bfloat(values):
    return lax.optimization_barrier(values.astype(jnp.bfloat16))

def encode(history, qkv_weight, out_weight, pool_weight):
    row_count = history.shape[0]
    widened = history.astype(jnp.float32)
    inverse = lax.rsqrt(lax.optimization_barrier(jnp.mean(widened * widened, axis=-1, keepdims=True)) + 1e-05)
    normed = to_bfloat(widened * inverse).reshape(row_count * S, D)
    packed = to_bfloat(jnp.dot(normed, qkv_weight, preferred_element_type=jnp.float32))
    packed = packed.reshape(row_count, S, 3, HEADS, HD)
    query_part = packed[:, :, 0].astype(jnp.float32)
    key_part = packed[:, :, 1].astype(jnp.float32)
    value_part = packed[:, :, 2].astype(jnp.float32)
    logits = jnp.einsum('rshd,rthd->rhst', query_part, key_part) / math.sqrt(HD)
    raised = jnp.exp(logits)
    attention = raised / lax.optimization_barrier(jnp.sum(raised, axis=-1, keepdims=True))
    attention_low = to_bfloat(attention)
    mixture = jnp.einsum('rhst,rthd->rshd', attention_low.astype(jnp.float32), value_part)
    mixture = to_bfloat(mixture).reshape(row_count * S, D)
    residual = widened.reshape(row_count * S, D) + jnp.dot(mixture, out_weight, preferred_element_type=jnp.float32)
    residual_low = to_bfloat(residual)
    active = jnp.tanh(jnp.dot(residual_low, pool_weight, preferred_element_type=jnp.float32))
    pooled = (lax.optimization_barrier(jnp.sum(active.reshape(row_count, S, D), axis=1)) / math.sqrt(S)).astype(jnp.bfloat16)
    stored = (widened, inverse, normed, query_part, key_part, value_part, attention, attention_low, mixture, residual_low, active)
    return (pooled, stored)

def backward(stored, grad_pooled, qkv_weight, out_weight, pool_weight):
    widened, inverse, normed, query_part, key_part, value_part, attention, attention_low, mixture, residual_low, active = stored
    row_count = grad_pooled.shape[0]
    grad_active = jnp.broadcast_to(grad_pooled[:, None, :] / math.sqrt(S), (row_count, S, D)).reshape(row_count * S, D)
    grad_pre = to_bfloat(grad_active * (1.0 - active * active))
    pool_grad = jnp.dot(residual_low.T, grad_pre, preferred_element_type=jnp.float32)
    grad_residual = jnp.dot(grad_pre, pool_weight.T, preferred_element_type=jnp.float32)
    grad_residual_low = to_bfloat(grad_residual)
    out_grad = jnp.dot(mixture.T, grad_residual_low, preferred_element_type=jnp.float32)
    grad_mixture = to_bfloat(jnp.dot(grad_residual_low, out_weight.T, preferred_element_type=jnp.float32))
    grad_mixture = grad_mixture.reshape(row_count, S, HEADS, HD).astype(jnp.float32)
    grad_attention = jnp.einsum('rshd,rthd->rhst', grad_mixture, value_part)
    grad_values = jnp.einsum('rhst,rshd->rthd', attention_low.astype(jnp.float32), grad_mixture)
    grad_logits = attention * (grad_attention - lax.optimization_barrier(jnp.sum(attention * grad_attention, axis=-1, keepdims=True))) / math.sqrt(HD)
    grad_logits = to_bfloat(grad_logits).astype(jnp.float32)
    grad_query = jnp.einsum('rhst,rthd->rshd', grad_logits, key_part)
    grad_keys = jnp.einsum('rhst,rshd->rthd', grad_logits, query_part)
    grad_packed = to_bfloat(jnp.stack([grad_query, grad_keys, grad_values], axis=2)).reshape(row_count * S, 3 * D)
    qkv_grad = jnp.dot(normed.T, grad_packed, preferred_element_type=jnp.float32)
    grad_normed = jnp.dot(grad_packed, qkv_weight.T, preferred_element_type=jnp.float32).reshape(row_count, S, D)
    grad_input = grad_residual.reshape(row_count, S, D) + inverse * grad_normed
    grad_input = grad_input - widened * inverse ** 3 * lax.optimization_barrier(jnp.mean(grad_normed * widened, axis=-1, keepdims=True))
    return (grad_input, qkv_grad, out_grad, pool_grad)

def score_cases(member_pooled, time_rows, case_weight, head_weight, risk_weight):
    cases = member_pooled.shape[0]
    hidden = to_bfloat(member_pooled.astype(jnp.float32) + time_rows[:, None, :]).reshape(cases * (K + 1), D)
    preact = jnp.dot(hidden, head_weight, preferred_element_type=jnp.float32)
    gated = jax.nn.sigmoid(preact)
    risk_score = lax.optimization_barrier(jnp.sum(preact * gated * risk_weight[None, :], axis=-1)).reshape(cases, K + 1)
    raised = jnp.exp(risk_score)
    shares = raised / lax.optimization_barrier(jnp.sum(raised, axis=-1, keepdims=True))
    is_case = (jnp.arange(K + 1) == 0).astype(jnp.float32)
    grad_risk = case_weight[:, None] * (shares - is_case[None, :])
    grad_preact = grad_risk.reshape(cases * (K + 1), 1) * risk_weight[None, :] * gated * (1.0 + preact * (1.0 - gated))
    grad_preact = to_bfloat(grad_preact)
    head_grad = jnp.dot(hidden.T, grad_preact, preferred_element_type=jnp.float32)
    grad_hidden = jnp.dot(grad_preact, head_weight.T, preferred_element_type=jnp.float32).reshape(cases, K + 1, D)
    return (grad_hidden, head_grad)

def reference(history, qkv_weight, out_weight, pool_weight, head_weight, risk_weight, time_table, case_rows, control_rows, buckets, case_weight):

    def pool_one(history_row):
        return encode(history_row[None], qkv_weight, out_weight, pool_weight)[0][0]
    pooled = lax.map(pool_one, history)
    owner_base = jnp.arange(CASES, dtype=jnp.int32) // C_DEV * R_DEV
    members = jnp.concatenate([(owner_base + case_rows.astype(jnp.int32))[:, None], control_rows.astype(jnp.int32)], axis=1)
    member_pooled = pooled[members]
    grad_hidden, head_grad = score_cases(member_pooled, time_table[buckets], case_weight, head_weight, risk_weight)
    grad_pooled = jnp.zeros((ROWS, D), jnp.float32).at[members.reshape(-1)].add(grad_hidden.reshape(-1, D))

    def row_step(totals, pair):
        history_row, grad_row = pair
        unused, stored = encode(history_row[None], qkv_weight, out_weight, pool_weight)
        grad_input, qkv_grad, out_grad, pool_grad = backward(stored, grad_row[None], qkv_weight, out_weight, pool_weight)
        return ((totals[0] + qkv_grad, totals[1] + out_grad, totals[2] + pool_grad), grad_input[0])
    zero_grads = (jnp.zeros((D, 3 * D), jnp.float32), jnp.zeros((D, D), jnp.float32), jnp.zeros((D, D), jnp.float32))
    sums, grad_input = lax.scan(row_step, zero_grads, (history, grad_pooled))
    return (grad_input, sums[0], sums[1], sums[2], head_grad)
```

```python
import math

import jax
import jax.numpy as jnp
from jax import lax
from jax.experimental import pallas as pl
from jax.experimental.pallas import tpu as pltpu
from jax.sharding import PartitionSpec as P

D = 1024
HD = 64
HEADS = 16
S = 128
K = 32
CAP = 4
NB = 128
R_DEV = 3
C_DEV = 3
DEVICES = 128
SLOTS = CAP * DEVICES
MEMBERS = SLOTS + 16

MESH = pl.DeviceIdType.MESH
F32 = jnp.float32
BF16 = jnp.bfloat16

WIDE = 512
GROUPS = (
    (0, 0, "zyx"),
    (0, 512, "yxz"),
    (1, 0, "xzy"),
    (1, 512, "zyx"),
    (2, 0, "yxz"),
    (2, 512, "xzy"),
)


def position():
    row = lax.axis_index("rows")
    col = lax.axis_index("cols")
    return {
        "z": lax.div(row, 4),
        "y": lax.rem(row, 4),
        "x": lax.div(col, 2),
        "core": lax.rem(col, 2),
    }


def device_at(place):
    return (place["z"] * 4 + place["y"], place["x"] * 2 + place["core"])


def moved(place, axis, step):
    return {**place, axis: lax.rem(place[axis] + step, 4)}


def remote(source, target, send_sem, recv_sem, place):
    return pltpu.make_async_remote_copy(
        src_ref=source,
        dst_ref=target,
        send_sem=send_sem,
        recv_sem=recv_sem,
        device_id=device_at(place),
        device_id_type=MESH,
    )


def greet(places):
    barrier = pltpu.get_barrier_semaphore()
    for place in places:
        pl.semaphore_signal(barrier, inc=1, device_id=device_at(place), device_id_type=MESH)
    pl.semaphore_wait(barrier, len(places))


def added(*parts):
    total = parts[0].astype(F32)
    for part in parts[1:]:
        total = total + part.astype(F32)
    return total


def grads_kernel(
    normed,
    mixture,
    residual_low,
    hidden,
    grad_packed,
    grad_residual_low,
    grad_pre,
    grad_preact,
    qkv_out,
    out_out,
    pool_out,
    head_out,
    part,
    swap,
    first,
    second_sum,
    second,
    third_sum,
    third,
    swap_send,
    swap_recv,
    first_send,
    first_recv,
    second_send,
    second_recv,
    third_send,
    third_recv,
):
    here = position()
    core = here["core"]
    twin = {**here, "core": 1 - core}
    greet([twin] + [moved(here, axis, step) for axis in "xyz" for step in (1, 2, 3)])

    slabs = (
        ((residual_low, grad_pre, 0, pool_out, 0), (hidden, grad_preact, 0, head_out, 0)),
        ((mixture, grad_residual_low, 0, out_out, 0), (normed, grad_packed, 2048, qkv_out, 2048)),
        ((normed, grad_packed, 0, qkv_out, 0), (normed, grad_packed, 1024, qkv_out, 1024)),
    )
    sends = []

    def send(copy):
        copy.start()
        sends.append(copy)

    def produce(g):
        slab, col0, order = GROUPS[g]

        def step(i, carry):
            z = lax.div(i, 2)
            n = lax.rem(i, 2)
            results = []
            for lhs, rhs, offset, _, _ in slabs[slab]:
                left = lhs[:, pl.ds(pl.multiple_of(z * 256, 256), 256)]
                right = rhs[:, pl.ds(pl.multiple_of(offset + col0 + n * 256, 256), 256)]
                results.append(
                    lax.dot_general(
                        left, right, (((0,), (0,)), ((), ())), preferred_element_type=F32
                    )
                )
            for y in range(4):
                for x in range(4):
                    for c in range(2):
                        row = y * 64 + x * 16 + c * 8
                        block = jnp.concatenate(
                            [r[row : row + 8] for r in results], axis=0
                        ).astype(BF16)
                        digit = {"z": z, "y": y, "x": x}
                        part[
                            g,
                            c,
                            digit[order[0]],
                            digit[order[1]],
                            digit[order[2]],
                            :,
                            pl.ds(pl.multiple_of(n * 256, 256), 256),
                        ] = block
            return carry

        lax.fori_loop(0, 8, step, 0)
        send(
            remote(part.at[g, 1 - core], swap.at[g], swap_send.at[g], swap_recv.at[g], twin)
        )

    def arrived(target, sem):
        remote(target, target, sem, sem, twin).wait_recv()

    def spread(axis, source, landing, send_sems, recv_sems):
        me = here[axis]
        right, left = moved(here, axis, 1), moved(here, axis, 3)
        far = lax.rem(me + 2, 4)
        for slot, digit, half, place in (
            (0, far, 0, right),
            (1, far, 2, left),
            (2, lax.rem(me + 1, 4), 2, right),
            (3, lax.rem(me + 3, 4), 0, left),
        ):
            send(
                remote(
                    source.at[digit, pl.ds(half, 2)],
                    landing.at[slot],
                    send_sems.at[slot],
                    recv_sems.at[slot],
                    place,
                )
            )

    def relay(axis, source, landing, send_sems, recv_sems):
        me = here[axis]
        right, left = moved(here, axis, 1), moved(here, axis, 3)
        for slot, came, digit, half, place in (
            (4, 0, lax.rem(me + 1, 4), 0, right),
            (5, 1, lax.rem(me + 3, 4), 2, left),
        ):
            arrived(landing.at[came], recv_sems.at[came])
            for k in range(2):
                source[digit, half + k] = added(
                    source[digit, half + k], landing[came, k]
                ).astype(BF16)
            send(
                remote(
                    source.at[digit, pl.ds(half, 2)],
                    landing.at[slot],
                    send_sems.at[slot],
                    recv_sems.at[slot],
                    place,
                )
            )

    def collect(axis, source, landing, recv_sems, target):
        me = here[axis]
        for slot in (2, 3, 4, 5):
            arrived(landing.at[slot], recv_sems.at[slot])
        for k in range(2):
            target[k] = added(source[me, k], landing[3, k], landing[4, k]).astype(BF16)
            target[2 + k] = added(source[me, 2 + k], landing[2, k], landing[5, k]).astype(BF16)

    def first_spread(g):
        arrived(swap.at[g], swap_recv.at[g])

        def step(i, carry):
            a = lax.div(i, 4)
            b = lax.rem(i, 4)
            part[g, core, a, b] = added(part[g, core, a, b], swap[g, a, b]).astype(BF16)
            return carry

        lax.fori_loop(0, 16, step, 0)
        spread(GROUPS[g][2][0], part.at[g, core], first.at[g], first_send.at[g], first_recv.at[g])

    def first_relay(g):
        relay(GROUPS[g][2][0], part.at[g, core], first.at[g], first_send.at[g], first_recv.at[g])

    def second_spread(g):
        order = GROUPS[g][2]
        collect(order[0], part.at[g, core], first.at[g], first_recv.at[g], second_sum.at[g])
        spread(order[1], second_sum.at[g], second.at[g], second_send.at[g], second_recv.at[g])

    def second_relay(g):
        relay(
            GROUPS[g][2][1], second_sum.at[g], second.at[g], second_send.at[g], second_recv.at[g]
        )

    def third_spread(g):
        order = GROUPS[g][2]
        collect(order[1], second_sum.at[g], second.at[g], second_recv.at[g], third_sum.at[g])
        axis = order[2]
        for step in (1, 2, 3):
            send(
                remote(
                    third_sum.at[g, lax.rem(here[axis] + step, 4)],
                    third.at[g, step - 1],
                    third_send.at[g, step - 1],
                    third_recv.at[g, step - 1],
                    moved(here, axis, step),
                )
            )

    def finish(g):
        slab, col0, order = GROUPS[g]
        for slot in range(3):
            arrived(third.at[g, slot], third_recv.at[g, slot])
        total = added(third_sum[g, here[order[2]]], third[g, 0], third[g, 1], third[g, 2])
        for t, (_, _, _, out, offset) in enumerate(slabs[slab]):
            out[:, offset + col0 : offset + col0 + WIDE] = total[8 * t : 8 * t + 8]

    stages = (
        produce,
        first_spread,
        first_relay,
        second_spread,
        second_relay,
        third_spread,
        finish,
    )
    for tick in range(len(GROUPS) + len(stages) - 1):
        for s, stage in enumerate(stages):
            if 0 <= tick - s < len(GROUPS):
                stage(tick - s)
    for copy in sends:
        copy.wait_send()


def weight_grads(
    normed, mixture, residual_low, hidden, grad_packed, grad_residual_low, grad_pre, grad_preact
):
    count = len(GROUPS)
    vmem = pl.BlockSpec(memory_space=pltpu.VMEM)
    return pl.pallas_call(
        grads_kernel,
        out_shape=(
            jax.ShapeDtypeStruct((8, 3 * D), F32),
            jax.ShapeDtypeStruct((8, D), F32),
            jax.ShapeDtypeStruct((8, D), F32),
            jax.ShapeDtypeStruct((8, D), F32),
        ),
        in_specs=[vmem] * 8,
        out_specs=(vmem,) * 4,
        scratch_shapes=[
            pltpu.VMEM((count, 2, 4, 4, 4, 16, WIDE), BF16),
            pltpu.VMEM((count, 4, 4, 4, 16, WIDE), BF16),
            pltpu.VMEM((count, 6, 2, 4, 16, WIDE), BF16),
            pltpu.VMEM((count, 4, 4, 16, WIDE), BF16),
            pltpu.VMEM((count, 6, 2, 16, WIDE), BF16),
            pltpu.VMEM((count, 4, 16, WIDE), BF16),
            pltpu.VMEM((count, 3, 16, WIDE), BF16),
            pltpu.SemaphoreType.DMA((count,)),
            pltpu.SemaphoreType.DMA((count,)),
            pltpu.SemaphoreType.DMA((count, 6)),
            pltpu.SemaphoreType.DMA((count, 6)),
            pltpu.SemaphoreType.DMA((count, 6)),
            pltpu.SemaphoreType.DMA((count, 6)),
            pltpu.SemaphoreType.DMA((count, 3)),
            pltpu.SemaphoreType.DMA((count, 3)),
        ],
        compiler_params=pltpu.CompilerParams(
            collective_id=1, has_side_effects=True, vmem_limit_bytes=52 * 2**20
        ),
    )(normed, mixture, residual_low, hidden, grad_packed, grad_residual_low, grad_pre, grad_preact)


def total_kernel(
    own, out, by_row, middle, by_col, row_send, row_recv, col_send, col_recv
):
    row = lax.axis_index("rows")
    col = lax.axis_index("cols")
    barrier = pltpu.get_barrier_semaphore()
    for step in range(1, 16):
        pl.semaphore_signal(
            barrier, inc=1, device_id=(lax.rem(row + step, 16), col), device_id_type=MESH
        )
    for step in range(1, 8):
        pl.semaphore_signal(
            barrier, inc=1, device_id=(row, lax.rem(col + step, 8)), device_id_type=MESH
        )
    pl.semaphore_wait(barrier, 22)

    def copy(source, landing, send_sems, recv_sems, step, target):
        return pltpu.make_async_remote_copy(
            src_ref=source,
            dst_ref=landing.at[step - 1],
            send_sem=send_sems.at[step - 1],
            recv_sem=recv_sems.at[step - 1],
            device_id=target,
            device_id_type=MESH,
        )

    first = [
        copy(own, by_row, row_send, row_recv, step, (lax.rem(row + step, 16), col))
        for step in range(1, 16)
    ]
    for one in first:
        one.start()
    for one in first:
        one.wait_recv()
    total = own[...]
    for step in range(15):
        total = total + by_row[step]
    middle[...] = total
    second = [
        copy(middle, by_col, col_send, col_recv, step, (row, lax.rem(col + step, 8)))
        for step in range(1, 8)
    ]
    for one in second:
        one.start()
    for one in second:
        one.wait_recv()
    for step in range(7):
        total = total + by_col[step]
    out[...] = total
    for one in first + second:
        one.wait_send()


def sum_devices(own):
    vmem = pl.BlockSpec(memory_space=pltpu.VMEM)
    return pl.pallas_call(
        total_kernel,
        out_shape=jax.ShapeDtypeStruct(own.shape, F32),
        in_specs=[vmem],
        out_specs=vmem,
        scratch_shapes=[
            pltpu.VMEM((15, *own.shape), F32),
            pltpu.VMEM(own.shape, F32),
            pltpu.VMEM((7, *own.shape), F32),
            pltpu.SemaphoreType.DMA((15,)),
            pltpu.SemaphoreType.DMA((15,)),
            pltpu.SemaphoreType.DMA((7,)),
            pltpu.SemaphoreType.DMA((7,)),
        ],
        compiler_params=pltpu.CompilerParams(collective_id=2, has_side_effects=True),
    )(own)


def encode(history, qkv_weight, out_weight, pool_weight):
    row_count = history.shape[0]
    widened = history.astype(jnp.float32)
    inverse = lax.rsqrt(jnp.mean(widened * widened, axis=-1, keepdims=True) + 1e-05)
    normed = (widened * inverse).astype(jnp.bfloat16).reshape(row_count * S, D)
    packed = jnp.dot(normed, qkv_weight, preferred_element_type=jnp.float32).astype(jnp.bfloat16)
    packed = packed.reshape(row_count, S, 3, HEADS, HD)
    query_part = packed[:, :, 0]
    key_part = packed[:, :, 1]
    value_part = packed[:, :, 2]
    logits = jnp.einsum(
        "rshd,rthd->rhst", query_part, key_part, preferred_element_type=jnp.float32
    ) / math.sqrt(HD)
    raised = jnp.exp(logits)
    attention = raised / jnp.sum(raised, axis=-1, keepdims=True)
    attention_low = attention.astype(jnp.bfloat16)
    mixture = jnp.einsum(
        "rhst,rthd->rshd", attention_low, value_part, preferred_element_type=jnp.float32
    )
    mixture = mixture.astype(jnp.bfloat16).reshape(row_count * S, D)
    residual = widened.reshape(row_count * S, D) + jnp.dot(
        mixture, out_weight, preferred_element_type=jnp.float32
    )
    residual_low = residual.astype(jnp.bfloat16)
    active = jnp.tanh(jnp.dot(residual_low, pool_weight, preferred_element_type=jnp.float32))
    pooled = (jnp.sum(active.reshape(row_count, S, D), axis=1) / math.sqrt(S)).astype(jnp.bfloat16)
    stored = (
        widened,
        inverse,
        normed,
        query_part,
        key_part,
        value_part,
        attention,
        attention_low,
        mixture,
        residual_low,
        active,
    )
    return (pooled, stored)


def backward(stored, grad_pooled, qkv_weight, out_weight, pool_weight):
    (
        widened,
        inverse,
        normed,
        query_part,
        key_part,
        value_part,
        attention,
        attention_low,
        mixture,
        residual_low,
        active,
    ) = stored
    row_count = grad_pooled.shape[0]
    grad_active = jnp.broadcast_to(
        grad_pooled[:, None, :] / math.sqrt(S), (row_count, S, D)
    ).reshape(row_count * S, D)
    grad_pre = (grad_active * (1.0 - active * active)).astype(jnp.bfloat16)
    grad_residual = jnp.einsum(
        "ne,de->nd", grad_pre, pool_weight, preferred_element_type=jnp.float32
    )
    grad_residual_low = grad_residual.astype(jnp.bfloat16)
    grad_mixture = jnp.einsum(
        "ne,de->nd", grad_residual_low, out_weight, preferred_element_type=jnp.float32
    )
    grad_mixture = grad_mixture.astype(jnp.bfloat16).reshape(row_count, S, HEADS, HD)
    grad_attention = jnp.einsum(
        "rshd,rthd->rhst", grad_mixture, value_part, preferred_element_type=jnp.float32
    )
    grad_values = jnp.einsum(
        "rhst,rshd->rthd", attention_low, grad_mixture, preferred_element_type=jnp.float32
    )
    grad_logits = (
        attention
        * (grad_attention - jnp.sum(attention * grad_attention, axis=-1, keepdims=True))
        / math.sqrt(HD)
    )
    grad_logits = grad_logits.astype(jnp.bfloat16)
    grad_query = jnp.einsum(
        "rhst,rthd->rshd", grad_logits, key_part, preferred_element_type=jnp.float32
    )
    grad_keys = jnp.einsum(
        "rhst,rshd->rthd", grad_logits, query_part, preferred_element_type=jnp.float32
    )
    grad_packed = (
        jnp.stack([grad_query, grad_keys, grad_values], axis=2)
        .astype(jnp.bfloat16)
        .reshape(row_count * S, 3 * D)
    )
    grad_normed = jnp.einsum(
        "ne,de->nd", grad_packed, qkv_weight, preferred_element_type=jnp.float32
    ).reshape(row_count, S, D)
    grad_input = grad_residual.reshape(row_count, S, D) + inverse * grad_normed
    grad_input = grad_input - widened * inverse**3 * jnp.mean(
        grad_normed * widened, axis=-1, keepdims=True
    )
    return (grad_input, grad_pre, grad_residual_low, grad_packed)


def iota(shape, dim):
    return lax.broadcasted_iota(jnp.int32, shape, dim)


def find_slots(facts, own, me):
    lane = iota((DEVICES, 128), 1)
    local = facts - (R_DEV * me).astype(F32)
    hit = (lane < C_DEV * K) & (local >= 0.0) & (local < float(R_DEV))
    hits = hit.astype(F32)
    before = (iota((128, 128), 0) < iota((128, 128), 1)).astype(BF16)
    order = jnp.dot(hits.astype(BF16), before, preferred_element_type=F32)
    case_of = jnp.where(lane < K, 0.0, jnp.where(lane < 2 * K, 1.0, 2.0))
    columns = [[], [], [], [], []]
    for j in range(CAP):
        chosen = jnp.where(hit & (order == float(j)), 1.0, 0.0)
        row = jnp.sum(chosen * local, axis=1, keepdims=True)
        case = jnp.sum(chosen * case_of, axis=1, keepdims=True)
        taken = jnp.sum(chosen, axis=1, keepdims=True)
        bucket = jnp.zeros_like(row)
        weight = jnp.zeros_like(row)
        for c in range(C_DEV):
            is_c = case == float(c)
            bucket = jnp.where(is_c, facts[:, 96 + c : 97 + c], bucket)
            weight = jnp.where(is_c, facts[:, 99 + c : 100 + c], weight)
        for column, values in zip(columns, (row, case, bucket, weight, taken)):
            column.append(values)
    own_case = iota((16, 1), 0).astype(F32)
    for column, values in zip(
        columns, (own[:, 0:1], own_case, own[:, 1:2], own[:, 2:3], own[:, 3:4])
    ):
        column.append(values)
    return [jnp.concatenate(column, axis=0) for column in columns]


def score_members(row, bucket, pooled, table3, head_weight, risk_weight):
    onehot = (iota((MEMBERS, NB), 1).astype(F32) == bucket).astype(BF16)
    times = jnp.dot(
        jnp.concatenate([onehot] * 3, axis=1), table3, preferred_element_type=F32
    )
    picked = jnp.where(
        row == 0.0, pooled[0:1], jnp.where(row == 1.0, pooled[1:2], pooled[2:3])
    )
    hidden = (picked + times).astype(BF16)
    preact = jnp.dot(hidden, head_weight, preferred_element_type=F32)
    gated = jax.nn.sigmoid(preact)
    score = jnp.sum(preact * gated * risk_weight, axis=1, keepdims=True)
    return hidden, preact, gated, jnp.exp(score)


def partial_sums(raised, case, taken, me):
    raised = jnp.where(taken > 0.0, raised, 0.0)
    lane = iota((DEVICES, 128), 1)
    mine = iota((DEVICES, 128), 0) == me
    sums = jnp.zeros((DEVICES, 128), F32)
    for c in range(C_DEV):
        share = jnp.zeros((DEVICES, 1), F32)
        for j in range(CAP):
            at = slice(j * DEVICES, (j + 1) * DEVICES)
            share = share + jnp.where(case[at] == float(c), raised[at], 0.0)
        share = share + jnp.where(mine, raised[SLOTS + c : SLOTS + c + 1], 0.0)
        sums = jnp.where(lane == c, share, sums)
    return sums.T[0:8]


def score_grads(sums, row, case, weight, taken, raised, preact, gated, risk_weight, head_weight, me):
    denominators = jnp.concatenate([sums, jnp.ones((120, 128), F32)], axis=0).T
    own = jnp.sum(
        jnp.where(iota((16, 128), 1) == me, jnp.concatenate([sums, jnp.ones((8, 128), F32)], axis=0), 0.0),
        axis=1,
        keepdims=True,
    )
    below = jnp.concatenate(
        [
            jnp.where(
                case[j * DEVICES : (j + 1) * DEVICES] == 0.0,
                denominators[:, 0:1],
                jnp.where(
                    case[j * DEVICES : (j + 1) * DEVICES] == 1.0,
                    denominators[:, 1:2],
                    denominators[:, 2:3],
                ),
            )
            for j in range(CAP)
        ]
        + [own],
        axis=0,
    )
    is_case = jnp.where(iota((MEMBERS, 1), 0) >= SLOTS, 1.0, 0.0)
    grad_risk = jnp.where(taken > 0.0, weight * (raised / below - is_case), 0.0)
    grad_preact = (grad_risk * risk_weight * gated * (1.0 + preact * (1.0 - gated))).astype(BF16)
    row_of = jnp.where(
        (iota((MEMBERS, 128), 1).astype(F32) == row) & (taken > 0.0), 1.0, 0.0
    ).astype(BF16)
    by_row = lax.dot_general(
        row_of, grad_preact, (((0,), (0,)), ((), ())), preferred_element_type=F32
    )[0:16]
    high = lax.reduce_precision(by_row, 8, 7)
    both = lax.dot_general(
        jnp.concatenate([high, by_row - high], axis=0).astype(BF16),
        head_weight,
        (((1,), (1,)), ((), ())),
        preferred_element_type=F32,
    )
    return grad_preact, both[0:16] + both[16:32]


def body(
    history,
    qkv_weight,
    out_weight,
    pool_weight,
    head_weight,
    risk_weight,
    time_table,
    case_rows,
    control_rows,
    buckets,
    case_weight,
):
    me = lax.axis_index("rows") * 8 + lax.axis_index("cols")
    mine = jnp.concatenate(
        [
            control_rows.reshape(C_DEV * K).astype(F32),
            buckets.astype(F32),
            case_weight,
            jnp.zeros((128 - C_DEV * (K + 2),), F32),
        ]
    )
    facts = lax.all_gather(mine[None], ("rows", "cols"), axis=0, tiled=True)
    own = jnp.stack(
        [case_rows.astype(F32), buckets.astype(F32), case_weight, jnp.ones((C_DEV,), F32)], axis=1
    )
    own = jnp.pad(own, ((0, 16 - C_DEV), (0, 124)))
    row, case, bucket, weight, taken = find_slots(facts, own, me)
    high = lax.reduce_precision(time_table, 8, 7)
    middle = lax.reduce_precision(time_table - high, 8, 7)
    table3 = jnp.concatenate([high, middle, time_table - high - middle], axis=0).astype(BF16)

    pooled, stored = encode(history, qkv_weight, out_weight, pool_weight)
    risk_row = risk_weight[None]
    hidden, preact, gated, raised = score_members(
        row, bucket, pooled.astype(F32), table3, head_weight, risk_row
    )
    sums = sum_devices(partial_sums(raised, case, taken, me))
    grad_preact, grad_pooled = score_grads(
        sums, row, case, weight, taken, raised, preact, gated, risk_row, head_weight, me
    )
    grad_input, grad_pre, grad_residual_low, grad_packed = backward(
        stored, grad_pooled[:R_DEV], qkv_weight, out_weight, pool_weight
    )
    normed, mixture, residual_low = stored[2], stored[8], stored[9]
    shares = weight_grads(
        normed, mixture, residual_low, hidden, grad_packed, grad_residual_low, grad_pre, grad_preact
    )
    return (grad_input, *shares)


def solution(mesh):
    in_specs = (
        P(("rows", "cols"), None, None),
        P(),
        P(),
        P(),
        P(),
        P(),
        P(),
        P(("rows", "cols")),
        P(("rows", "cols"), None),
        P(("rows", "cols")),
        P(("rows", "cols")),
    )
    out_specs = (
        P(("rows", "cols"), None, None),
        P(("rows", "cols"), None),
        P(("rows", "cols"), None),
        P(("rows", "cols"), None),
        P(("rows", "cols"), None),
    )
    return jax.shard_map(body, mesh=mesh, in_specs=in_specs, out_specs=out_specs, check_vma=False)
```

```python
import math

import jax
import jax.numpy as jnp
from jax import lax
from jax.experimental import pallas as pl
from jax.experimental.pallas import tpu as pltpu
from jax.sharding import PartitionSpec as P

D = 1024
HD = 64
HEADS = 16
S = 128
K = 32
CAP = 4
NB = 128
R_DEV = 3
C_DEV = 3
TOKENS = R_DEV * S
DEVICES = 128
SLOTS = CAP * DEVICES
MEMBERS = SLOTS + 16
PAIRS = HEADS // 2

MESH = pl.DeviceIdType.MESH
F32 = jnp.float32
BF16 = jnp.bfloat16

WIDE = 512
GROUPS = (
    (0, 0, "zyx"),
    (0, 512, "yxz"),
    (1, 0, "xzy"),
    (1, 512, "zyx"),
    (2, 0, "yxz"),
    (2, 512, "xzy"),
)
COUNT = len(GROUPS)
SPARE = 3


def device_at(place):
    return (place["z"] * 4 + place["y"], place["x"] * 2 + place["core"])


def moved(place, axis, step):
    return {**place, axis: lax.rem(place[axis] + step, 4)}


def remote(source, target, send_sem, recv_sem, device):
    return pltpu.make_async_remote_copy(
        src_ref=source,
        dst_ref=target,
        send_sem=send_sem,
        recv_sem=recv_sem,
        device_id=device,
        device_id_type=MESH,
    )


def added(*parts):
    total = parts[0].astype(F32)
    for part in parts[1:]:
        total = total + part.astype(F32)
    return total


def iota(shape, dim):
    return lax.broadcasted_iota(jnp.int32, shape, dim)


def dot(a, b, contract_a=1, contract_b=0):
    return lax.dot_general(
        a, b, (((contract_a,), (contract_b,)), ((), ())), preferred_element_type=F32
    )


def block(i, size):
    return pl.ds(pl.multiple_of(i * size, size), size)


def loop(count, step, unroll=1):
    def run(i, carry):
        step(i)
        return carry

    lax.fori_loop(0, count, run, 0, unroll=unroll)


def find_slots(facts, own, me):
    lane = iota((DEVICES, 128), 1)
    local = facts - (R_DEV * me).astype(F32)
    hit = (lane < C_DEV * K) & (local >= 0.0) & (local < float(R_DEV))
    hits = jnp.where(hit, 1.0, 0.0)
    before = jnp.where(iota((128, 128), 0) < iota((128, 128), 1), 1.0, 0.0).astype(BF16)
    order = dot(hits.astype(BF16), before)
    case_of = jnp.where(lane < K, 0.0, jnp.where(lane < 2 * K, 1.0, 2.0))
    columns = [[], [], [], [], []]
    for j in range(CAP):
        chosen = jnp.where(order == float(j), hits, 0.0)
        row = jnp.sum(chosen * local, axis=1, keepdims=True)
        case = jnp.sum(chosen * case_of, axis=1, keepdims=True)
        taken = jnp.sum(chosen, axis=1, keepdims=True)
        bucket = jnp.zeros_like(row)
        weight = jnp.zeros_like(row)
        for c in range(C_DEV):
            is_c = case == float(c)
            bucket = jnp.where(is_c, facts[:, 96 + c : 97 + c], bucket)
            weight = jnp.where(is_c, facts[:, 99 + c : 100 + c], weight)
        for column, values in zip(columns, (row, case, bucket, weight, taken)):
            column.append(values)
    own_case = iota((16, 1), 0).astype(F32)
    for column, values in zip(
        columns, (own[:, 0:1], own_case, own[:, 1:2], own[:, 2:3], own[:, 3:4])
    ):
        column.append(values)
    return [jnp.concatenate(column, axis=0) for column in columns]


def partial_sums(raised, case, taken, me):
    raised = jnp.where(taken > 0.0, raised, 0.0)
    lane = iota((DEVICES, 128), 1)
    mine = iota((DEVICES, 128), 0) == me
    sums = jnp.zeros((DEVICES, 128), F32)
    for c in range(C_DEV):
        share = jnp.zeros((DEVICES, 1), F32)
        for j in range(CAP):
            at = slice(j * DEVICES, (j + 1) * DEVICES)
            share = share + jnp.where(case[at] == float(c), raised[at], 0.0)
        share = share + jnp.where(mine, raised[SLOTS + c : SLOTS + c + 1], 0.0)
        sums = jnp.where(lane == c, share, sums)
    return sums.T[0:8]


def risk_grads(sums, case, weight, taken, raised, me):
    denominators = jnp.concatenate([sums, jnp.ones((120, 128), F32)], axis=0).T
    wide = jnp.concatenate([sums, jnp.ones((8, 128), F32)], axis=0)
    own = jnp.sum(jnp.where(iota((16, 128), 1) == me, wide, 0.0), axis=1, keepdims=True)
    below = []
    for j in range(CAP):
        of = case[j * DEVICES : (j + 1) * DEVICES]
        below.append(
            jnp.where(
                of == 0.0,
                denominators[:, 0:1],
                jnp.where(of == 1.0, denominators[:, 1:2], denominators[:, 2:3]),
            )
        )
    below = jnp.concatenate(below + [own], axis=0)
    is_case = jnp.where(iota((MEMBERS, 1), 0) >= SLOTS, 1.0, 0.0)
    return jnp.where(taken > 0.0, weight * (raised / below - is_case), 0.0)


def kernel(
    history_in,
    qkv_in,
    out_in,
    pool_in,
    head_in,
    table_in,
    risk_ref,
    control_ref,
    case_rows,
    buckets,
    case_weight,
    grad_input_out,
    qkv_out,
    out_out,
    pool_out,
    head_out,
    history,
    qkv_weight,
    out_weight,
    pool_weight,
    head_weight,
    table,
    normed,
    inverse,
    packed,
    attention,
    mixture,
    residual_low,
    slope,
    pooled,
    hidden,
    head_slope,
    grad_preact,
    grad_pre,
    grad_residual,
    grad_residual_low,
    grad_mixture,
    grad_packed,
    facts,
    facts_in,
    facts_mine,
    sums_own,
    sums_middle,
    sums_row,
    sums_col,
    part,
    swap,
    first,
    second_sum,
    second,
    third_sum,
    third,
    load_sem,
    store_sem,
    fact_col_send,
    fact_col_recv,
    fact_row_send,
    fact_row_recv,
    sum_row_send,
    sum_row_recv,
    sum_col_send,
    sum_col_recv,
    swap_send,
    swap_recv,
    first_send,
    first_recv,
    second_send,
    second_recv,
    third_send,
    third_recv,
):
    row = lax.axis_index("rows")
    col = lax.axis_index("cols")
    here = {"z": lax.div(row, 4), "y": lax.rem(row, 4), "x": lax.div(col, 2), "core": lax.rem(col, 2)}
    core = here["core"]
    twin = device_at({**here, "core": 1 - core})
    me = row * 8 + col
    row_peers = [(lax.rem(row + step, 16), col) for step in range(1, 16)]
    col_peers = [(row, lax.rem(col + step, 8)) for step in range(1, 8)]
    sends = []

    def send(copy):
        copy.start()
        sends.append(copy)

    def arrived(target, sem):
        remote(target, target, sem, sem, twin).wait_recv()

    loads = [
        pltpu.make_async_copy(source, target, load_sem.at[i])
        for i, (source, target) in enumerate(
            (
                (history_in, history),
                (qkv_in, qkv_weight),
                (table_in, table),
                (out_in, out_weight),
                (pool_in, pool_weight),
                (head_in, head_weight),
            )
        )
    ]
    for copy in loads:
        copy.start()
    barrier = pltpu.get_barrier_semaphore()
    for peer in row_peers + col_peers:
        pl.semaphore_signal(barrier, inc=1, device_id=peer, device_id_type=MESH)
    pl.semaphore_wait(barrier, len(row_peers) + len(col_peers))

    lane = iota((1, 128), 1)
    controls = control_ref[...].astype(F32)
    mine = jnp.concatenate(
        [controls[c : c + 1] for c in range(C_DEV)] + [jnp.zeros((1, 128 - C_DEV * K), F32)], axis=1
    )
    wide_lane, wide_row = iota((16, 128), 1), iota((16, 128), 0)
    own = jnp.where((wide_lane == 3) & (wide_row < C_DEV), 1.0, 0.0)
    for c in range(C_DEV):
        bucket, weight = buckets[c].astype(F32), case_weight[c]
        mine = jnp.where(lane == 96 + c, bucket, mine)
        mine = jnp.where(lane == 99 + c, weight, mine)
        for place, value in enumerate((case_rows[c].astype(F32), bucket, weight)):
            own = jnp.where((wide_lane == place) & (wide_row == c), value, own)
    facts_mine[...] = jnp.broadcast_to(mine, (8, 128))
    for i, peer in enumerate(col_peers):
        send(
            remote(facts_mine, facts_in.at[i], fact_col_send.at[i], fact_col_recv.at[i], peer)
        )

    loads[0].wait()

    def normalise(r):
        rows = block(r, S)
        x = history[rows, :].astype(F32)
        inv = lax.rsqrt(jnp.mean(x * x, axis=1, keepdims=True) + 1e-05)
        inverse[rows, :] = inv
        normed[rows, :] = (x * inv).astype(BF16)

    loop(R_DEV, normalise)
    loads[1].wait()

    def project(n):
        packed[:, block(n, 256)] = dot(normed[...], qkv_weight[:, block(n, 256)]).astype(BF16)

    loop(12, project)

    sub = iota((8, 128), 0)
    tile = jnp.where(sub == col, facts_mine[...], 0.0)
    for i in range(7):
        arrived(facts_in.at[i], fact_col_recv.at[i])
        tile = jnp.where(sub == lax.rem(col + 7 - i, 8), facts_in[i], tile)
    facts[row] = tile
    for i, peer in enumerate(row_peers):
        send(
            remote(facts.at[row], facts.at[row], fact_row_send.at[i], fact_row_recv.at[i], peer)
        )

    low_half = iota((S, 128), 1) < HD

    def halves(values):
        zero = jnp.zeros_like(values)
        return jnp.concatenate(
            [jnp.where(low_half, values, zero), jnp.where(low_half, zero, values)], axis=0
        )

    def joined(values):
        return jnp.where(low_half, values[:S], values[S:])

    def attend_one(r, p):
        rows = block(r, S)
        query = packed[rows, block(p, 128)]
        key = packed[rows, block(PAIRS + p, 128)]
        value = packed[rows, block(2 * PAIRS + p, 128)]
        raised = jnp.exp(dot(query, halves(key), 1, 1) * (1.0 / math.sqrt(HD)))
        low = jnp.concatenate(
            [
                raised[:, :S] / jnp.sum(raised[:, :S], axis=1, keepdims=True),
                raised[:, S:] / jnp.sum(raised[:, S:], axis=1, keepdims=True),
            ],
            axis=1,
        ).astype(BF16)
        attention[r, p] = low
        mixture[rows, block(p, 128)] = dot(low, halves(value)).astype(BF16)

    def attend(i):
        for k in range(4):
            attend_one(lax.div(i, 2), lax.rem(i, 2) * 4 + k)

    loop(2 * R_DEV, attend)
    loads[3].wait()

    def add_residual(n):
        cols = block(n, 256)
        residual = history[:, cols].astype(F32) + dot(mixture[...], out_weight[:, cols])
        residual_low[:, cols] = residual.astype(BF16)

    loop(4, add_residual)
    loads[4].wait()
    sub16 = iota((16, 256), 0)

    def pool(n):
        cols = block(n, 256)
        active = jnp.tanh(dot(residual_low[...], pool_weight[:, cols]))
        slope[:, cols] = (1.0 - active * active) * (1.0 / math.sqrt(S))
        rows = jnp.zeros((16, 256), F32)
        for r in range(R_DEV):
            total = jnp.sum(active[r * S : (r + 1) * S], axis=0, keepdims=True)
            rows = jnp.where(sub16 == r, total * (1.0 / math.sqrt(S)), rows)
        pooled[:, cols] = rows.astype(BF16).astype(F32)

    loop(4, pool)

    for i in range(15):
        source = lax.rem(row + 15 - i, 16)
        arrived(facts.at[source], fact_row_recv.at[i])
    at_row, case, bucket, weight, taken = find_slots(facts[...].reshape(DEVICES, 128), own, me)
    loads[2].wait()
    loads[5].wait()
    onehot = jnp.where(iota((MEMBERS, NB), 1).astype(F32) == bucket, 1.0, 0.0).astype(BF16)
    onehots = jnp.concatenate([onehot] * 3, axis=1)

    def embed(n):
        cols = block(n, 256)
        times = table[:, cols]
        high = times.astype(BF16)
        middle = (times - high.astype(F32)).astype(BF16)
        low = (times - high.astype(F32) - middle.astype(F32)).astype(BF16)
        rows = pooled[:, cols]
        picked = jnp.where(at_row == 0.0, rows[0:1], jnp.where(at_row == 1.0, rows[1:2], rows[2:3]))
        hidden[:, cols] = (
            picked + dot(onehots, jnp.concatenate([high, middle, low], axis=0))
        ).astype(BF16)

    loop(4, embed)

    def score(n, total):
        cols = block(n, 256)
        preact = dot(hidden[...], head_weight[:, cols])
        gated = jax.nn.sigmoid(preact)
        risk = risk_ref[:, cols]
        head_slope[:, cols] = risk * gated * (1.0 + preact * (1.0 - gated))
        return total + jnp.sum(preact * gated * risk, axis=1, keepdims=True)

    raised = jnp.exp(lax.fori_loop(0, 4, score, jnp.zeros((MEMBERS, 1), F32)))

    sums = partial_sums(raised, case, taken, me)
    sums_own[...] = sums
    for i, peer in enumerate(row_peers):
        send(remote(sums_own, sums_row.at[i], sum_row_send.at[i], sum_row_recv.at[i], peer))
    for i in range(15):
        arrived(sums_row.at[i], sum_row_recv.at[i])
        sums = sums + sums_row[i]
    sums_middle[...] = sums
    for i, peer in enumerate(col_peers):
        send(remote(sums_middle, sums_col.at[i], sum_col_send.at[i], sum_col_recv.at[i], peer))
    for i in range(7):
        arrived(sums_col.at[i], sum_col_recv.at[i])
        sums = sums + sums_col[i]

    grad_risk = risk_grads(sums, case, weight, taken, raised, me)
    row_of = jnp.where(
        (iota((MEMBERS, 128), 1).astype(F32) == at_row) & (taken > 0.0), 1.0, 0.0
    ).astype(BF16)

    def score_grad(n):
        cols = block(n, 256)
        grad = (grad_risk * head_slope[:, cols]).astype(BF16)
        grad_preact[:, cols] = grad
        pooled[:, cols] = dot(row_of, grad, 0, 0)[0:16]

    loop(4, score_grad)
    by_row = pooled[...]
    high = by_row.astype(BF16)
    low = (by_row - high.astype(F32)).astype(BF16)
    by_row = jnp.concatenate([high, low], axis=0)

    def pool_grad(n):
        both = dot(by_row, head_weight[block(n, 256), :], 1, 1)
        grad = both[0:16] + both[16:32]
        cols = block(n, 256)
        for r in range(R_DEV):
            rows = slice(r * S, (r + 1) * S)
            grad_pre[rows, cols] = (grad[r : r + 1] * slope[rows, cols]).astype(BF16)

    loop(4, pool_grad)

    slabs = (
        ((residual_low, grad_pre, 0, pool_out, 0), (hidden, grad_preact, 0, head_out, 0)),
        ((mixture, grad_residual_low, 0, out_out, 0), (normed, grad_packed, 2048, qkv_out, 2048)),
        ((normed, grad_packed, 0, qkv_out, 0), (normed, grad_packed, 1024, qkv_out, 1024)),
    )
    swaps = {}

    def produce(g):
        slab, col0, order = GROUPS[g]
        spare = COUNT + g % SPARE
        if g >= SPARE:
            swaps[g - SPARE].wait_send()

        def step(i):
            z = lax.div(i, 2)
            n = lax.rem(i, 2)
            results = [
                dot(lhs[:, block(z, 256)], rhs[:, block((offset + col0) // 256 + n, 256)], 0, 0)
                for lhs, rhs, offset, _, _ in slabs[slab]
            ]
            for y in range(4):
                for x in range(4):
                    for c in range(2):
                        at = y * 64 + x * 16 + c * 8
                        digit = {"z": z, "y": y, "x": x}
                        part[
                            jnp.where(core == c, g, spare),
                            digit[order[0]],
                            digit[order[1]],
                            digit[order[2]],
                            :,
                            block(n, 256),
                        ] = jnp.concatenate([r[at : at + 8] for r in results], axis=0).astype(BF16)

        loop(8, step)
        swaps[g] = remote(part.at[spare], swap.at[g], swap_send.at[g], swap_recv.at[g], twin)
        swaps[g].start()

    def spread(axis, source, landing, send_sems, recv_sems):
        at = here[axis]
        right, left = device_at(moved(here, axis, 1)), device_at(moved(here, axis, 3))
        far = lax.rem(at + 2, 4)
        for slot, digit, half, device in (
            (0, far, 0, right),
            (1, far, 2, left),
            (2, lax.rem(at + 1, 4), 2, right),
            (3, lax.rem(at + 3, 4), 0, left),
        ):
            send(
                remote(
                    source.at[digit, pl.ds(half, 2)],
                    landing.at[slot],
                    send_sems.at[slot],
                    recv_sems.at[slot],
                    device,
                )
            )

    def relay(axis, source, landing, send_sems, recv_sems):
        at = here[axis]
        right, left = device_at(moved(here, axis, 1)), device_at(moved(here, axis, 3))
        for slot, came, digit, half, device in (
            (4, 0, lax.rem(at + 1, 4), 0, right),
            (5, 1, lax.rem(at + 3, 4), 2, left),
        ):
            arrived(landing.at[came], recv_sems.at[came])
            for k in range(2):
                source[digit, half + k] = added(
                    source[digit, half + k], landing[came, k]
                ).astype(BF16)
            send(
                remote(
                    source.at[digit, pl.ds(half, 2)],
                    landing.at[slot],
                    send_sems.at[slot],
                    recv_sems.at[slot],
                    device,
                )
            )

    def collect(axis, source, landing, recv_sems, target):
        at = here[axis]
        for slot in (2, 3, 4, 5):
            arrived(landing.at[slot], recv_sems.at[slot])
        for k in range(2):
            target[k] = added(source[at, k], landing[3, k], landing[4, k]).astype(BF16)
            target[2 + k] = added(source[at, 2 + k], landing[2, k], landing[5, k]).astype(BF16)

    def first_spread(g):
        arrived(swap.at[g], swap_recv.at[g])

        def step(i):
            a, b = lax.div(i, 4), lax.rem(i, 4)
            part[g, a, b] = added(part[g, a, b], swap[g, a, b]).astype(BF16)

        loop(16, step)
        spread(GROUPS[g][2][0], part.at[g], first.at[g], first_send.at[g], first_recv.at[g])

    def first_relay(g):
        relay(GROUPS[g][2][0], part.at[g], first.at[g], first_send.at[g], first_recv.at[g])

    def second_spread(g):
        order = GROUPS[g][2]
        collect(order[0], part.at[g], first.at[g], first_recv.at[g], second_sum.at[g])
        spread(order[1], second_sum.at[g], second.at[g], second_send.at[g], second_recv.at[g])

    def second_relay(g):
        relay(
            GROUPS[g][2][1], second_sum.at[g], second.at[g], second_send.at[g], second_recv.at[g]
        )

    def third_spread(g):
        order = GROUPS[g][2]
        collect(order[1], second_sum.at[g], second.at[g], second_recv.at[g], third_sum.at[g])
        axis = order[2]
        for step in (1, 2, 3):
            send(
                remote(
                    third_sum.at[g, lax.rem(here[axis] + step, 4)],
                    third.at[g, step - 1],
                    third_send.at[g, step - 1],
                    third_recv.at[g, step - 1],
                    device_at(moved(here, axis, step)),
                )
            )

    def finish(g):
        slab, col0, order = GROUPS[g]
        for slot in range(3):
            arrived(third.at[g, slot], third_recv.at[g, slot])
        total = added(third_sum[g, here[order[2]]], third[g, 0], third[g, 1], third[g, 2])
        for t, (_, _, _, out, offset) in enumerate(slabs[slab]):
            out[:, offset + col0 : offset + col0 + WIDE] = total[8 * t : 8 * t + 8]

    def back_residual():
        def step(n):
            cols = block(n, 256)
            grad = dot(grad_pre[...], pool_weight[cols, :], 1, 1)
            grad_residual[:, cols] = grad
            grad_residual_low[:, cols] = grad.astype(BF16)

        loop(4, step)

    def back_mixture():
        def step(n):
            cols = block(n, 256)
            grad_mixture[:, cols] = dot(grad_residual_low[...], out_weight[cols, :], 1, 1).astype(BF16)

        loop(4, step)

    def back_attend_one(r, p):
        rows = block(r, S)
        query = packed[rows, block(p, 128)]
        key = packed[rows, block(PAIRS + p, 128)]
        value = packed[rows, block(2 * PAIRS + p, 128)]
        grad = grad_mixture[rows, block(p, 128)]
        low = attention[r, p]
        weights = low.astype(F32)
        grad_attention = dot(grad, halves(value), 1, 1)
        product = weights * grad_attention
        inner = [
            jnp.sum(product[:, :S], axis=1, keepdims=True),
            jnp.sum(product[:, S:], axis=1, keepdims=True),
        ]
        scale = 1.0 / math.sqrt(HD)
        grad_logits = jnp.concatenate(
            [
                weights[:, :S] * (grad_attention[:, :S] - inner[0]) * scale,
                weights[:, S:] * (grad_attention[:, S:] - inner[1]) * scale,
            ],
            axis=1,
        ).astype(BF16)
        grad_packed[rows, block(p, 128)] = dot(grad_logits, halves(key)).astype(BF16)
        grad_packed[rows, block(PAIRS + p, 128)] = joined(dot(grad_logits, query, 0, 0)).astype(BF16)
        grad_packed[rows, block(2 * PAIRS + p, 128)] = joined(dot(low, grad, 0, 0)).astype(BF16)

    def back_attend(r):
        def step(i):
            for k in range(4):
                back_attend_one(r, i * 4 + k)

        loop(2, step)

    def back_normed(n):
        cols = slice(n * 256, (n + 1) * 256)
        head_slope[0:TOKENS, cols] = dot(grad_packed[...], qkv_weight[cols, :], 1, 1)

    stores = []

    def back_input():
        for r in range(R_DEV):
            rows = slice(r * S, (r + 1) * S)
            grad = head_slope[rows, :]
            x = history[rows, :].astype(F32)
            inv = inverse[rows, :]
            mean = jnp.mean(grad * x, axis=1, keepdims=True)
            head_slope[rows, :] = grad_residual[rows, :] + inv * grad - x * (inv * inv * inv * mean)
            stores.append(
                pltpu.make_async_copy(head_slope.at[rows], grad_input_out.at[rows], store_sem.at[r])
            )
            stores[-1].start()

    a, b, c, d, e, f, g = (
        produce,
        first_spread,
        first_relay,
        second_spread,
        second_relay,
        third_spread,
        finish,
    )
    plan = (
        (a, 0), (a, 1), (back_residual,), (b, 0), (b, 1), (back_mixture,), (c, 0), (c, 1),
        (back_attend, 0), (d, 0), (d, 1), (back_attend, 1), (e, 0), (e, 1), (back_attend, 2),
        (a, 2), (f, 0), (f, 1), (a, 3), (b, 2), (a, 4), (b, 3), (c, 2), (a, 5),
        (b, 4), (c, 3), (d, 2), (g, 0), (g, 1), (back_normed, 0), (b, 5), (c, 4), (d, 3), (e, 2),
        (back_normed, 1), (c, 5), (d, 4), (e, 3), (f, 2), (back_normed, 2), (d, 5), (e, 4), (f, 3),
        (g, 2), (back_normed, 3), (e, 5), (f, 4), (g, 3), (back_input,), (f, 5), (g, 4), (g, 5),
    )
    for stage, *at in plan:
        stage(*at)

    for g in range(COUNT - SPARE, COUNT):
        swaps[g].wait_send()
    for copy in sends:
        copy.wait_send()
    for copy in stores:
        copy.wait()


def body(
    history,
    qkv_weight,
    out_weight,
    pool_weight,
    head_weight,
    risk_weight,
    time_table,
    case_rows,
    control_rows,
    buckets,
    case_weight,
):
    vmem = pl.BlockSpec(memory_space=pltpu.VMEM)
    smem = pl.BlockSpec(memory_space=pltpu.SMEM)
    hbm = pl.BlockSpec(memory_space=pl.ANY)
    dma = pltpu.SemaphoreType.DMA
    grad_input, *shares = pl.pallas_call(
        kernel,
        out_shape=(
            jax.ShapeDtypeStruct((TOKENS, D), F32),
            jax.ShapeDtypeStruct((8, 3 * D), F32),
            jax.ShapeDtypeStruct((8, D), F32),
            jax.ShapeDtypeStruct((8, D), F32),
            jax.ShapeDtypeStruct((8, D), F32),
        ),
        in_specs=[hbm] * 6 + [vmem] * 2 + [smem] * 3,
        out_specs=(hbm,) + (vmem,) * 4,
        scratch_shapes=[
            pltpu.VMEM((TOKENS, D), BF16),
            pltpu.VMEM((D, 3 * D), BF16),
            pltpu.VMEM((D, D), BF16),
            pltpu.VMEM((D, D), BF16),
            pltpu.VMEM((D, D), BF16),
            pltpu.VMEM((NB, D), F32),
            pltpu.VMEM((TOKENS, D), BF16),
            pltpu.VMEM((TOKENS, 1), F32),
            pltpu.VMEM((TOKENS, 3 * D), BF16),
            pltpu.VMEM((R_DEV, PAIRS, S, 2 * S), BF16),
            pltpu.VMEM((TOKENS, D), BF16),
            pltpu.VMEM((TOKENS, D), BF16),
            pltpu.VMEM((TOKENS, D), F32),
            pltpu.VMEM((16, D), F32),
            pltpu.VMEM((MEMBERS, D), BF16),
            pltpu.VMEM((MEMBERS, D), F32),
            pltpu.VMEM((MEMBERS, D), BF16),
            pltpu.VMEM((TOKENS, D), BF16),
            pltpu.VMEM((TOKENS, D), F32),
            pltpu.VMEM((TOKENS, D), BF16),
            pltpu.VMEM((TOKENS, D), BF16),
            pltpu.VMEM((TOKENS, 3 * D), BF16),
            pltpu.VMEM((16, 8, 128), F32),
            pltpu.VMEM((7, 8, 128), F32),
            pltpu.VMEM((8, 128), F32),
            pltpu.VMEM((8, 128), F32),
            pltpu.VMEM((8, 128), F32),
            pltpu.VMEM((15, 8, 128), F32),
            pltpu.VMEM((7, 8, 128), F32),
            pltpu.VMEM((COUNT + SPARE, 4, 4, 4, 16, WIDE), BF16),
            pltpu.VMEM((COUNT, 4, 4, 4, 16, WIDE), BF16),
            pltpu.VMEM((COUNT, 6, 2, 4, 16, WIDE), BF16),
            pltpu.VMEM((COUNT, 4, 4, 16, WIDE), BF16),
            pltpu.VMEM((COUNT, 6, 2, 16, WIDE), BF16),
            pltpu.VMEM((COUNT, 4, 16, WIDE), BF16),
            pltpu.VMEM((COUNT, 3, 16, WIDE), BF16),
            dma((6,)),
            dma((3,)),
            dma((7,)),
            dma((7,)),
            dma((15,)),
            dma((15,)),
            dma((15,)),
            dma((15,)),
            dma((7,)),
            dma((7,)),
            dma((COUNT,)),
            dma((COUNT,)),
            dma((COUNT, 6)),
            dma((COUNT, 6)),
            dma((COUNT, 6)),
            dma((COUNT, 6)),
            dma((COUNT, 3)),
            dma((COUNT, 3)),
        ],
        compiler_params=pltpu.CompilerParams(
            collective_id=1, has_side_effects=True, vmem_limit_bytes=61 * 2**20
        ),
    )(
        history.reshape(TOKENS, D),
        qkv_weight,
        out_weight,
        pool_weight,
        head_weight,
        time_table,
        risk_weight[None],
        control_rows,
        case_rows,
        buckets,
        case_weight,
    )
    return (grad_input.reshape(R_DEV, S, D), *shares)


def solution(mesh):
    in_specs = (
        P(("rows", "cols"), None, None),
        P(),
        P(),
        P(),
        P(),
        P(),
        P(),
        P(("rows", "cols")),
        P(("rows", "cols"), None),
        P(("rows", "cols")),
        P(("rows", "cols")),
    )
    out_specs = (
        P(("rows", "cols"), None, None),
        P(("rows", "cols"), None),
        P(("rows", "cols"), None),
        P(("rows", "cols"), None),
        P(("rows", "cols"), None),
    )
    return jax.shard_map(body, mesh=mesh, in_specs=in_specs, out_specs=out_specs, check_vma=False)
```

```python
import math

import jax
import jax.numpy as jnp
from jax import lax
from jax.experimental import pallas as pl
from jax.experimental.pallas import tpu as pltpu
from jax.sharding import PartitionSpec as P

D = 1024
HD = 64
HEADS = 16
S = 128
K = 32
CAP = 4
NB = 128
R_DEV = 3
C_DEV = 3
TOKENS = R_DEV * S
DEVICES = 128
SLOTS = CAP * DEVICES
MEMBERS = SLOTS + 16
PAIRS = HEADS // 2

MESH = pl.DeviceIdType.MESH
F32 = jnp.float32
BF16 = jnp.bfloat16

GROUPS = (
    (0, 0, 512, "zyx"),
    (0, 512, 256, "yxz"),
    (0, 768, 256, "xzy"),
    (1, 0, 512, "yxz"),
    (2, 0, 512, "xzy"),
    (1, 512, 256, "zyx"),
    (2, 512, 256, "zyx"),
    (1, 768, 256, "yxz"),
    (2, 768, 256, "xzy"),
)
COUNT = len(GROUPS)


def device_at(place):
    return (place["z"] * 4 + place["y"], place["x"] * 2 + place["core"])


def moved(place, axis, step):
    return {**place, axis: lax.rem(place[axis] + step, 4)}


def remote(source, target, send_sem, recv_sem, device):
    return pltpu.make_async_remote_copy(
        src_ref=source,
        dst_ref=target,
        send_sem=send_sem,
        recv_sem=recv_sem,
        device_id=device,
        device_id_type=MESH,
    )


def added(*parts):
    total = parts[0].astype(F32)
    for part in parts[1:]:
        total = total + part.astype(F32)
    return total


def iota(shape, dim):
    return lax.broadcasted_iota(jnp.int32, shape, dim)


def dot(a, b, contract_a=1, contract_b=0):
    return lax.dot_general(
        a, b, (((contract_a,), (contract_b,)), ((), ())), preferred_element_type=F32
    )


def block(i, size):
    return pl.ds(pl.multiple_of(i * size, size), size)


def loop(count, step, unroll=1):
    def run(i, carry):
        step(i)
        return carry

    lax.fori_loop(0, count, run, 0, unroll=unroll)


def find_slots(facts, own, me):
    lane = iota((DEVICES, 128), 1)
    local = facts - (R_DEV * me).astype(F32)
    hit = (lane < C_DEV * K) & (local >= 0.0) & (local < float(R_DEV))
    hits = jnp.where(hit, 1.0, 0.0)
    before = jnp.where(iota((128, 128), 0) < iota((128, 128), 1), 1.0, 0.0).astype(BF16)
    order = dot(hits.astype(BF16), before)
    case_of = jnp.where(lane < K, 0.0, jnp.where(lane < 2 * K, 1.0, 2.0))
    columns = [[], [], [], [], []]
    for j in range(CAP):
        chosen = jnp.where(order == float(j), hits, 0.0)
        row = jnp.sum(chosen * local, axis=1, keepdims=True)
        case = jnp.sum(chosen * case_of, axis=1, keepdims=True)
        taken = jnp.sum(chosen, axis=1, keepdims=True)
        bucket = jnp.zeros_like(row)
        weight = jnp.zeros_like(row)
        for c in range(C_DEV):
            is_c = case == float(c)
            bucket = jnp.where(is_c, facts[:, 96 + c : 97 + c], bucket)
            weight = jnp.where(is_c, facts[:, 99 + c : 100 + c], weight)
        for column, values in zip(columns, (row, case, bucket, weight, taken)):
            column.append(values)
    own_case = iota((16, 1), 0).astype(F32)
    for column, values in zip(
        columns, (own[:, 0:1], own_case, own[:, 1:2], own[:, 2:3], own[:, 3:4])
    ):
        column.append(values)
    return [jnp.concatenate(column, axis=0) for column in columns]


def partial_sums(raised, case, taken, me):
    raised = jnp.where(taken > 0.0, raised, 0.0)
    lane = iota((DEVICES, 128), 1)
    mine = iota((DEVICES, 128), 0) == me
    sums = jnp.zeros((DEVICES, 128), F32)
    for c in range(C_DEV):
        share = jnp.zeros((DEVICES, 1), F32)
        for j in range(CAP):
            at = slice(j * DEVICES, (j + 1) * DEVICES)
            share = share + jnp.where(case[at] == float(c), raised[at], 0.0)
        share = share + jnp.where(mine, raised[SLOTS + c : SLOTS + c + 1], 0.0)
        sums = jnp.where(lane == c, share, sums)
    return sums.T[0:8]


def risk_grads(sums, case, weight, taken, raised, me):
    denominators = jnp.concatenate([sums, jnp.ones((120, 128), F32)], axis=0).T
    wide = jnp.concatenate([sums, jnp.ones((8, 128), F32)], axis=0)
    own = jnp.sum(jnp.where(iota((16, 128), 1) == me, wide, 0.0), axis=1, keepdims=True)
    below = []
    for j in range(CAP):
        of = case[j * DEVICES : (j + 1) * DEVICES]
        below.append(
            jnp.where(
                of == 0.0,
                denominators[:, 0:1],
                jnp.where(of == 1.0, denominators[:, 1:2], denominators[:, 2:3]),
            )
        )
    below = jnp.concatenate(below + [own], axis=0)
    is_case = jnp.where(iota((MEMBERS, 1), 0) >= SLOTS, 1.0, 0.0)
    return jnp.where(taken > 0.0, weight * (raised / below - is_case), 0.0)


def kernel(
    history_in,
    qkv_in,
    out_in,
    pool_in,
    head_in,
    table_in,
    risk_ref,
    control_ref,
    case_rows,
    buckets,
    case_weight,
    grad_input_out,
    qkv_out,
    out_out,
    pool_out,
    head_out,
    history,
    qkv_weight,
    out_weight,
    pool_weight,
    head_weight,
    table,
    normed,
    inverse,
    packed,
    attention,
    mixture,
    residual_low,
    slope,
    pooled,
    hidden,
    head_slope,
    grad_preact,
    grad_residual,
    grad_packed,
    normed_t,
    mixture_t,
    residual_t,
    facts,
    facts_in,
    facts_mine,
    sums_own,
    sums_middle,
    sums_row,
    sums_col,
    load_sem,
    store_sem,
    fact_col_send,
    fact_col_recv,
    fact_row_send,
    fact_row_recv,
    sum_row_send,
    sum_row_recv,
    sum_col_send,
    sum_col_recv,
    swap_send,
    swap_recv,
    first_send,
    first_recv,
    second_send,
    second_recv,
    third_send,
    third_recv,
    *buffers,
):
    part, swap, first, second_sum, second, third_sum, third = (
        buffers[i * COUNT : (i + 1) * COUNT] for i in range(7)
    )
    grad_pre, grad_residual_low, grad_mixture = residual_low, normed, mixture
    row = lax.axis_index("rows")
    col = lax.axis_index("cols")
    here = {"z": lax.div(row, 4), "y": lax.rem(row, 4), "x": lax.div(col, 2), "core": lax.rem(col, 2)}
    core = here["core"]
    twin = device_at({**here, "core": 1 - core})
    me = row * 8 + col
    row_peers = [(lax.rem(row + step, 16), col) for step in range(1, 16)]
    col_peers = [(row, lax.rem(col + step, 8)) for step in range(1, 8)]
    sends = []

    def send(copy):
        copy.start()
        sends.append(copy)

    def arrived(target, sem):
        remote(target, target, sem, sem, twin).wait_recv()

    loads = [
        pltpu.make_async_copy(source, target, load_sem.at[i])
        for i, (source, target) in enumerate(
            (
                (history_in, history),
                (qkv_in.at[:, 0:D], qkv_weight.at[:, 0:D]),
                (qkv_in.at[:, D : 2 * D], qkv_weight.at[:, D : 2 * D]),
                (qkv_in.at[:, 2 * D : 3 * D], qkv_weight.at[:, 2 * D : 3 * D]),
                (out_in, out_weight),
                (pool_in, pool_weight),
                (head_in, head_weight),
                (table_in, table),
            )
        )
    ]
    for copy in loads:
        copy.start()
    barrier = pltpu.get_barrier_semaphore()
    for peer in row_peers + col_peers:
        pl.semaphore_signal(barrier, inc=1, device_id=peer, device_id_type=MESH)
    lane = iota((1, 128), 1)
    controls = control_ref[...].astype(F32)
    mine = jnp.concatenate(
        [controls[c : c + 1] for c in range(C_DEV)] + [jnp.zeros((1, 128 - C_DEV * K), F32)], axis=1
    )
    wide_lane, wide_row = iota((16, 128), 1), iota((16, 128), 0)
    own = jnp.where((wide_lane == 3) & (wide_row < C_DEV), 1.0, 0.0)
    for c in range(C_DEV):
        bucket, weight = buckets[c].astype(F32), case_weight[c]
        mine = jnp.where(lane == 96 + c, bucket, mine)
        mine = jnp.where(lane == 99 + c, weight, mine)
        for place, value in enumerate((case_rows[c].astype(F32), bucket, weight)):
            own = jnp.where((wide_lane == place) & (wide_row == c), value, own)
    facts_mine[...] = jnp.broadcast_to(mine, (8, 128))

    loads[0].wait()

    def normalise(r):
        rows = block(r, S)
        x = history[rows, :].astype(F32)
        inv = lax.rsqrt(jnp.mean(x * x, axis=1, keepdims=True) + 1e-05)
        inverse[rows, :] = inv
        normed[rows, :] = (x * inv).astype(BF16)

    loop(R_DEV, normalise)
    pl.semaphore_wait(barrier, len(row_peers) + len(col_peers))
    for i, peer in enumerate(col_peers):
        send(
            remote(facts_mine, facts_in.at[i], fact_col_send.at[i], fact_col_recv.at[i], peer)
        )
    for n in range(3):
        loads[1 + n].wait()
        cols = slice(n * D, (n + 1) * D)
        packed[:, cols] = dot(normed[...], qkv_weight[:, cols]).astype(BF16)

    sub = iota((8, 128), 0)
    tile = jnp.where(sub == col, facts_mine[...], 0.0)
    for i in range(7):
        arrived(facts_in.at[i], fact_col_recv.at[i])
        tile = jnp.where(sub == lax.rem(col + 7 - i, 8), facts_in[i], tile)
    facts[row] = tile
    for i, peer in enumerate(row_peers):
        send(
            remote(facts.at[row], facts.at[row], fact_row_send.at[i], fact_row_recv.at[i], peer)
        )

    low_half = iota((S, 128), 1) < HD

    def halves(values):
        zero = jnp.zeros_like(values)
        return jnp.concatenate(
            [jnp.where(low_half, values, zero), jnp.where(low_half, zero, values)], axis=0
        )

    def joined(values):
        return jnp.where(low_half, values[:S], values[S:])

    def attend(r):
        rows = block(r, S)
        for p in range(PAIRS):
            query = packed[rows, p * 128 : p * 128 + 128]
            key = packed[rows, D + p * 128 : D + p * 128 + 128]
            value = packed[rows, 2 * D + p * 128 : 2 * D + p * 128 + 128]
            raised = jnp.exp(dot(halves(key), query, 1, 1) * (1.0 / math.sqrt(HD)))
            low = jnp.concatenate(
                [
                    raised[:S] * (1.0 / jnp.sum(raised[:S], axis=0, keepdims=True)),
                    raised[S:] * (1.0 / jnp.sum(raised[S:], axis=0, keepdims=True)),
                ],
                axis=0,
            ).astype(BF16)
            attention[r, p] = low
            mixture[rows, p * 128 : p * 128 + 128] = dot(low, halves(value), 0, 0).astype(BF16)

    loop(R_DEV, attend)
    loads[4].wait()

    def add_residual(n):
        cols = block(n, 512)
        residual = history[:, cols].astype(F32) + dot(mixture[...], out_weight[:, cols])
        residual_low[:, cols] = residual.astype(BF16)

    loop(2, add_residual)
    loads[5].wait()
    sub16 = iota((16, 512), 0)

    def pool(n):
        cols = block(n, 512)
        active = jnp.tanh(dot(residual_low[...], pool_weight[:, cols]))
        slope[:, cols] = (1.0 - active * active) * (1.0 / math.sqrt(S))
        rows = jnp.zeros((16, 512), F32)
        for r in range(R_DEV):
            total = jnp.sum(active[r * S : (r + 1) * S], axis=0, keepdims=True)
            rows = jnp.where(sub16 == r, total * (1.0 / math.sqrt(S)), rows)
        pooled[:, cols] = rows.astype(BF16).astype(F32)

    loop(2, pool)

    for i in range(15):
        source = lax.rem(row + 15 - i, 16)
        arrived(facts.at[source], fact_row_recv.at[i])
    at_row, case, bucket, weight, taken = find_slots(facts[...].reshape(DEVICES, 128), own, me)
    loads[6].wait()
    loads[7].wait()
    onehot = jnp.where(iota((MEMBERS, NB), 1).astype(F32) == bucket, 1.0, 0.0).astype(BF16)
    onehots = jnp.concatenate([onehot] * 3, axis=1)

    def embed(n):
        cols = block(n, 512)
        times = table[:, cols]
        high = times.astype(BF16)
        middle = (times - high.astype(F32)).astype(BF16)
        low = (times - high.astype(F32) - middle.astype(F32)).astype(BF16)
        rows = pooled[:, cols]
        picked = jnp.where(at_row == 0.0, rows[0:1], jnp.where(at_row == 1.0, rows[1:2], rows[2:3]))
        hidden[:, cols] = (
            picked + dot(onehots, jnp.concatenate([high, middle, low], axis=0))
        ).astype(BF16)

    loop(2, embed)

    def score(n, total):
        cols = block(n, 512)
        preact = dot(hidden[...], head_weight[:, cols])
        gated = jax.nn.sigmoid(preact)
        risk = risk_ref[:, cols]
        head_slope[:, cols] = risk * gated * (1.0 + preact * (1.0 - gated))
        return total + jnp.sum(preact * gated * risk, axis=1, keepdims=True)

    raised = jnp.exp(lax.fori_loop(0, 2, score, jnp.zeros((MEMBERS, 1), F32)))

    sums = partial_sums(raised, case, taken, me)
    sums_own[...] = sums
    for i, peer in enumerate(row_peers):
        send(remote(sums_own, sums_row.at[i], sum_row_send.at[i], sum_row_recv.at[i], peer))
    normed_t[...] = normed[...].T
    mixture_t[...] = mixture[...].T
    for i in range(15):
        arrived(sums_row.at[i], sum_row_recv.at[i])
        sums = sums + sums_row[i]
    sums_middle[...] = sums
    for i, peer in enumerate(col_peers):
        send(remote(sums_middle, sums_col.at[i], sum_col_send.at[i], sum_col_recv.at[i], peer))
    residual_t[...] = residual_low[...].T
    for i in range(7):
        arrived(sums_col.at[i], sum_col_recv.at[i])
        sums = sums + sums_col[i]

    grad_risk = risk_grads(sums, case, weight, taken, raised, me)
    row_of = jnp.where(
        (iota((MEMBERS, 128), 1).astype(F32) == at_row) & (taken > 0.0), 1.0, 0.0
    ).astype(BF16)

    def score_grad(n):
        cols = block(n, 512)
        grad = (grad_risk * head_slope[:, cols]).astype(BF16)
        grad_preact[:, cols] = grad
        pooled[:, cols] = dot(row_of, grad, 0, 0)[0:16]

    loop(2, score_grad)
    by_row = pooled[...]
    high = by_row.astype(BF16)
    low = (by_row - high.astype(F32)).astype(BF16)
    by_row = jnp.concatenate([high, low], axis=0)

    def pool_grad(n):
        both = dot(by_row, head_weight[block(n, 512), :], 1, 1)
        grad = both[0:16] + both[16:32]
        cols = block(n, 512)
        for r in range(R_DEV):
            rows = slice(r * S, (r + 1) * S)
            grad_pre[rows, cols] = (grad[r : r + 1] * slope[rows, cols]).astype(BF16)

    loop(2, pool_grad)

    slabs = (
        ((residual_t, 1, grad_pre, 0, pool_out, 0), (hidden, 0, grad_preact, 0, head_out, 0)),
        (
            (mixture_t, 1, grad_residual_low, 0, out_out, 0),
            (normed_t, 1, grad_packed, 2 * D, qkv_out, 2 * D),
        ),
        ((normed_t, 1, grad_packed, 0, qkv_out, 0), (normed_t, 1, grad_packed, D, qkv_out, D)),
    )

    def produce(g):
        slab, col0, width, order = GROUPS[g]
        results = [
            dot(lhs[...], rhs[:, offset + col0 : offset + col0 + width], contract, 0).reshape(
                4, 4, 4, 2, 8, width
            )
            for lhs, contract, rhs, offset, _, _ in slabs[slab]
        ]
        for c in range(2):
            for z in range(4):
                for y in range(4):
                    values = jnp.concatenate(
                        [result[z, y, :, c] for result in results], axis=1
                    ).astype(BF16)
                    if order == "zyx":
                        part[g][c, z, y] = values
                    elif order == "yxz":
                        part[g][c, y, :, z] = values
                    else:
                        part[g][c, :, z, y] = values
        send(remote(part[g].at[1 - core], swap[g], swap_send.at[g], swap_recv.at[g], twin))

    def ring(g):
        at = here[GROUPS[g][3][0]]
        return at, lax.rem(at + 1, 4), lax.rem(at + 2, 4), lax.rem(at + 3, 4)

    def send_first(g, slot, digit, half, step):
        send(
            remote(
                part[g].at[core, digit, pl.ds(half, 2)],
                first[g].at[slot],
                first_send.at[g, slot],
                first_recv.at[g, slot],
                device_at(moved(here, GROUPS[g][3][0], step)),
            )
        )

    def first_spread(g):
        at, right, far, left = ring(g)
        arrived(swap[g], swap_recv.at[g])
        for b in range(4):
            part[g][core, far, b] = added(part[g][core, far, b], swap[g][far, b]).astype(BF16)
        send_first(g, 0, far, 0, 1)
        send_first(g, 1, far, 2, 3)
        for b in range(2):
            part[g][core, right, 2 + b] = added(
                part[g][core, right, 2 + b], swap[g][right, 2 + b]
            ).astype(BF16)
            part[g][core, left, b] = added(part[g][core, left, b], swap[g][left, b]).astype(BF16)
        send_first(g, 2, right, 2, 1)
        send_first(g, 3, left, 0, 3)

    def first_relay(g):
        at, right, far, left = ring(g)
        for slot, came, digit, half, step in ((4, 0, right, 0, 1), (5, 1, left, 2, 3)):
            arrived(first[g].at[came], first_recv.at[g, came])
            for k in range(2):
                b = half + k
                part[g][core, digit, b] = added(
                    part[g][core, digit, b], swap[g][digit, b], first[g][came, k]
                ).astype(BF16)
            send_first(g, slot, digit, half, step)

    def second_spread(g):
        at = ring(g)[0]
        for slot in (2, 3, 4, 5):
            arrived(first[g].at[slot], first_recv.at[g, slot])
        for b in range(4):
            one, other = (3, 4) if b < 2 else (2, 5)
            second_sum[g][b] = added(
                part[g][core, at, b], swap[g][at, b], first[g][one, b % 2], first[g][other, b % 2]
            ).astype(BF16)
        direct(GROUPS[g][3][1], second_sum[g], second[g], second_send.at[g], second_recv.at[g])

    def direct(axis, source, landing, send_sems, recv_sems):
        for step in (2, 1, 3):
            send(
                remote(
                    source.at[lax.rem(here[axis] + step, 4)],
                    landing.at[step - 1],
                    send_sems.at[step - 1],
                    recv_sems.at[step - 1],
                    device_at(moved(here, axis, step)),
                )
            )

    def third_spread(g):
        at = here[GROUPS[g][3][1]]
        for slot in range(3):
            arrived(second[g].at[slot], second_recv.at[g, slot])
        third_sum[g][...] = added(second_sum[g][at], second[g][0], second[g][1], second[g][2]).astype(
            BF16
        )
        direct(GROUPS[g][3][2], third_sum[g], third[g], third_send.at[g], third_recv.at[g])

    def finish(g):
        slab, col0, width, order = GROUPS[g]
        for slot in range(3):
            arrived(third[g].at[slot], third_recv.at[g, slot])
        total = added(third_sum[g][here[order[2]]], third[g][0], third[g][1], third[g][2])
        for t, (_, _, _, _, out, offset) in enumerate(slabs[slab]):
            out[:, offset + col0 : offset + col0 + width] = total[8 * t : 8 * t + 8]

    def back_residual():
        def step(n):
            cols = block(n, 512)
            grad = dot(grad_pre[...], pool_weight[cols, :], 1, 1)
            grad_residual[:, cols] = grad
            grad_residual_low[:, cols] = grad.astype(BF16)

        loop(2, step)

    def back_mixture():
        def step(n):
            cols = block(n, 512)
            grad_mixture[:, cols] = dot(grad_residual_low[...], out_weight[cols, :], 1, 1).astype(BF16)

        loop(2, step)

    def back_attend_one(r, p):
        rows = slice(r * S, (r + 1) * S)
        query_at, key_at, value_at = (slice(i * D + p * 128, i * D + p * 128 + 128) for i in range(3))
        query, key, value = packed[rows, query_at], packed[rows, key_at], packed[rows, value_at]
        grad = grad_mixture[rows, query_at]
        low = attention[r, p]
        weights = low.astype(F32)
        grad_attention = dot(halves(value), grad, 1, 1)
        product = weights * grad_attention
        scale = 1.0 / math.sqrt(HD)
        grad_logits = jnp.concatenate(
            [
                weights[at]
                * (grad_attention[at] - jnp.sum(product[at], axis=0, keepdims=True))
                * scale
                for at in (slice(0, S), slice(S, 2 * S))
            ],
            axis=0,
        ).astype(BF16)
        grad_packed[rows, query_at] = dot(grad_logits, halves(key), 0, 0).astype(BF16)
        grad_packed[rows, key_at] = joined(dot(grad_logits, query)).astype(BF16)
        grad_packed[rows, value_at] = joined(dot(low, grad)).astype(BF16)

    def back_attend(first_pair, pairs):
        for r in range(R_DEV):
            for p in range(first_pair, first_pair + pairs):
                back_attend_one(r, p)

    def back_normed(n):
        cols = slice(n * 512, (n + 1) * 512)
        head_slope[0:TOKENS, cols] = dot(grad_packed[...], qkv_weight[cols, :], 1, 1)

    stores = []

    def back_input():
        for r in range(R_DEV):
            rows = slice(r * S, (r + 1) * S)
            grad = head_slope[rows, :]
            x = history[rows, :].astype(F32)
            inv = inverse[rows, :]
            mean = jnp.mean(grad * x, axis=1, keepdims=True)
            head_slope[rows, :] = grad_residual[rows, :] + inv * grad - x * (inv * inv * inv * mean)
            stores.append(
                pltpu.make_async_copy(head_slope.at[rows], grad_input_out.at[rows], store_sem.at[r])
            )
            stores[-1].start()

    a, b, c, d, e, f = produce, first_spread, first_relay, second_spread, third_spread, finish
    plan = (
        (a, 1), (a, 2), (a, 0), (back_residual,), (b, 1), (b, 2), (back_mixture,), (b, 0), (back_attend, 0, 4), (a, 3), (a, 4), (c, 1), (c, 2), (c, 0), (back_attend, 4, 2), (b, 3), (b, 4), (a, 5), (a, 6), (back_attend, 6, 2), (b, 5), (b, 6), (a, 7), (a, 8), (d, 1), (d, 2), (d, 0), (c, 3), (c, 4), (b, 7), (b, 8), (c, 5), (c, 6), (back_normed, 0), (d, 3), (d, 4), (c, 7), (c, 8), (e, 1), (e, 2), (e, 0), (back_normed, 1), (d, 5), (d, 6), (e, 3), (e, 4), (d, 7), (d, 8), (back_input,), (e, 5), (e, 6), (f, 1), (f, 2), (f, 0), (e, 7), (e, 8), (f, 3), (f, 4), (f, 5), (f, 6), (f, 7), (f, 8),
    )
    for stage, *at in plan:
        stage(*at)

    for copy in sends:
        copy.wait_send()
    for copy in stores:
        copy.wait()


def deliver(results):
    steps = 4

    def copy_kernel(*refs):
        for source, target in zip(refs[: len(results)], refs[len(results) :]):
            target[...] = source[...]

    specs = [pl.BlockSpec((TOKENS // steps, D), lambda i: (i, 0))]
    for result in results[1:]:
        specs.append(pl.BlockSpec((8, result.shape[1] // steps), lambda i: (0, i)))
    return pl.pallas_call(
        copy_kernel,
        grid=(steps,),
        out_shape=tuple(jax.ShapeDtypeStruct(x.shape, x.dtype) for x in results),
        in_specs=specs,
        out_specs=tuple(specs),
    )(*results)


def body(
    history,
    qkv_weight,
    out_weight,
    pool_weight,
    head_weight,
    risk_weight,
    time_table,
    case_rows,
    control_rows,
    buckets,
    case_weight,
):
    vmem = pl.BlockSpec(memory_space=pltpu.VMEM)
    smem = pl.BlockSpec(memory_space=pltpu.SMEM)
    hbm = pl.BlockSpec(memory_space=pl.ANY)
    dma = pltpu.SemaphoreType.DMA
    results = pl.pallas_call(
        kernel,
        out_shape=(
            jax.ShapeDtypeStruct((TOKENS, D), F32),
            jax.ShapeDtypeStruct((8, 3 * D), F32),
            jax.ShapeDtypeStruct((8, D), F32),
            jax.ShapeDtypeStruct((8, D), F32),
            jax.ShapeDtypeStruct((8, D), F32),
        ),
        in_specs=[hbm] * 6 + [vmem] * 2 + [smem] * 3,
        out_specs=(hbm,) + (vmem,) * 4,
        scratch_shapes=[
            pltpu.VMEM((TOKENS, D), BF16),
            pltpu.VMEM((D, 3 * D), BF16),
            pltpu.VMEM((D, D), BF16),
            pltpu.VMEM((D, D), BF16),
            pltpu.VMEM((D, D), BF16),
            pltpu.VMEM((NB, D), F32),
            pltpu.VMEM((TOKENS, D), BF16),
            pltpu.VMEM((TOKENS, 1), F32),
            pltpu.VMEM((TOKENS, 3 * D), BF16),
            pltpu.VMEM((R_DEV, PAIRS, 2 * S, S), BF16),
            pltpu.VMEM((TOKENS, D), BF16),
            pltpu.VMEM((TOKENS, D), BF16),
            pltpu.VMEM((TOKENS, D), F32),
            pltpu.VMEM((16, D), F32),
            pltpu.VMEM((MEMBERS, D), BF16),
            pltpu.VMEM((MEMBERS, D), F32),
            pltpu.VMEM((MEMBERS, D), BF16),
            pltpu.VMEM((TOKENS, D), F32),
            pltpu.VMEM((TOKENS, 3 * D), BF16),
            pltpu.VMEM((D, TOKENS), BF16),
            pltpu.VMEM((D, TOKENS), BF16),
            pltpu.VMEM((D, TOKENS), BF16),
            pltpu.VMEM((16, 8, 128), F32),
            pltpu.VMEM((7, 8, 128), F32),
            pltpu.VMEM((8, 128), F32),
            pltpu.VMEM((8, 128), F32),
            pltpu.VMEM((8, 128), F32),
            pltpu.VMEM((15, 8, 128), F32),
            pltpu.VMEM((7, 8, 128), F32),
            dma((8,)),
            dma((3,)),
            dma((7,)),
            dma((7,)),
            dma((15,)),
            dma((15,)),
            dma((15,)),
            dma((15,)),
            dma((7,)),
            dma((7,)),
            dma((COUNT,)),
            dma((COUNT,)),
            dma((COUNT, 6)),
            dma((COUNT, 6)),
            dma((COUNT, 3)),
            dma((COUNT, 3)),
            dma((COUNT, 3)),
            dma((COUNT, 3)),
        ]
        + [
            pltpu.VMEM((*shape, 16, group[2]), BF16)
            for shape in (
                (2, 4, 4, 4),
                (4, 4, 4),
                (6, 2, 4),
                (4, 4),
                (3, 4),
                (4,),
                (3,),
            )
            for group in GROUPS
        ],
        compiler_params=pltpu.CompilerParams(
            collective_id=1, has_side_effects=True, vmem_limit_bytes=62 * 2**20
        ),
    )(
        history.reshape(TOKENS, D),
        qkv_weight,
        out_weight,
        pool_weight,
        head_weight,
        time_table,
        risk_weight[None],
        control_rows,
        case_rows,
        buckets,
        case_weight,
    )
    grad_input, *shares = deliver(results)
    return (grad_input.reshape(R_DEV, S, D), *shares)


def solution(mesh):
    in_specs = (
        P(("rows", "cols"), None, None),
        P(),
        P(),
        P(),
        P(),
        P(),
        P(),
        P(("rows", "cols")),
        P(("rows", "cols"), None),
        P(("rows", "cols")),
        P(("rows", "cols")),
    )
    out_specs = (
        P(("rows", "cols"), None, None),
        P(("rows", "cols"), None),
        P(("rows", "cols"), None),
        P(("rows", "cols"), None),
        P(("rows", "cols"), None),
    )
    return jax.shard_map(body, mesh=mesh, in_specs=in_specs, out_specs=out_specs, check_vma=False)
```

```python
import math

import jax
import jax.numpy as jnp
from jax import lax
from jax.experimental import pallas as pl
from jax.experimental.pallas import tpu as pltpu
from jax.sharding import PartitionSpec as P

D = 1024
HD = 64
HEADS = 16
S = 128
K = 32
CAP = 4
NB = 128
R_DEV = 3
C_DEV = 3
TOKENS = R_DEV * S
DEVICES = 128
SLOTS = CAP * DEVICES
MEMBERS = SLOTS + 16
PAIRS = HEADS // 2

MESH = pl.DeviceIdType.MESH
F32 = jnp.float32
BF16 = jnp.bfloat16

GROUPS = (
    (("head", 0), ("head", 512), 512, "zyx"),
    (("pool", 0), ("pool", 512), 512, "yxz"),
    (("out", 0), ("out", 512), 512, "xzy"),
    (("qkv", 0), ("qkv", D), 256, "zyx"),
    (("qkv", 256), ("qkv", D + 256), 256, "yxz"),
    (("qkv", 2 * D), ("qkv", 2 * D + 256), 256, "xzy"),
    (("qkv", 512), ("qkv", D + 512), 256, "zyx"),
    (("qkv", 768), ("qkv", D + 768), 256, "yxz"),
    (("qkv", 2 * D + 512), ("qkv", 2 * D + 768), 256, "xzy"),
)
COUNT = len(GROUPS)


def device_at(place):
    return (place["z"] * 4 + place["y"], place["x"] * 2 + place["core"])


def moved(place, axis, step):
    return {**place, axis: lax.rem(place[axis] + step, 4)}


def remote(source, target, send_sem, recv_sem, device):
    return pltpu.make_async_remote_copy(
        src_ref=source,
        dst_ref=target,
        send_sem=send_sem,
        recv_sem=recv_sem,
        device_id=device,
        device_id_type=MESH,
    )


def added(*parts):
    total = parts[0].astype(F32)
    for part in parts[1:]:
        total = total + part.astype(F32)
    return total


def iota(shape, dim):
    return lax.broadcasted_iota(jnp.int32, shape, dim)


def dot(a, b, contract_a=1, contract_b=0):
    return lax.dot_general(
        a, b, (((contract_a,), (contract_b,)), ((), ())), preferred_element_type=F32
    )


def block(i, size):
    return pl.ds(pl.multiple_of(i * size, size), size)


def loop(count, step, unroll=1):
    def run(i, carry):
        step(i)
        return carry

    lax.fori_loop(0, count, run, 0, unroll=unroll)


def find_slots(facts, own, me):
    lane = iota((DEVICES, 128), 1)
    local = facts - (R_DEV * me).astype(F32)
    hit = (lane < C_DEV * K) & (local >= 0.0) & (local < float(R_DEV))
    hits = jnp.where(hit, 1.0, 0.0)
    before = jnp.where(iota((128, 128), 0) < iota((128, 128), 1), 1.0, 0.0).astype(BF16)
    order = dot(hits.astype(BF16), before)
    case_of = jnp.where(lane < K, 0.0, jnp.where(lane < 2 * K, 1.0, 2.0))
    columns = [[], [], [], [], []]
    for j in range(CAP):
        chosen = jnp.where(order == float(j), hits, 0.0)
        row = jnp.sum(chosen * local, axis=1, keepdims=True)
        case = jnp.sum(chosen * case_of, axis=1, keepdims=True)
        taken = jnp.sum(chosen, axis=1, keepdims=True)
        bucket = jnp.zeros_like(row)
        weight = jnp.zeros_like(row)
        for c in range(C_DEV):
            is_c = case == float(c)
            bucket = jnp.where(is_c, facts[:, 96 + c : 97 + c], bucket)
            weight = jnp.where(is_c, facts[:, 99 + c : 100 + c], weight)
        for column, values in zip(columns, (row, case, bucket, weight, taken)):
            column.append(values)
    own_case = iota((16, 1), 0).astype(F32)
    for column, values in zip(
        columns, (own[:, 0:1], own_case, own[:, 1:2], own[:, 2:3], own[:, 3:4])
    ):
        column.append(values)
    return [jnp.concatenate(column, axis=0) for column in columns]


def partial_sums(raised, case, taken, me):
    raised = jnp.where(taken > 0.0, raised, 0.0)
    lane = iota((DEVICES, 128), 1)
    mine = iota((DEVICES, 128), 0) == me
    sums = jnp.zeros((DEVICES, 128), F32)
    for c in range(C_DEV):
        share = jnp.zeros((DEVICES, 1), F32)
        for j in range(CAP):
            at = slice(j * DEVICES, (j + 1) * DEVICES)
            share = share + jnp.where(case[at] == float(c), raised[at], 0.0)
        share = share + jnp.where(mine, raised[SLOTS + c : SLOTS + c + 1], 0.0)
        sums = jnp.where(lane == c, share, sums)
    return sums.T[0:4]


def risk_grads(sums, case, weight, taken, raised, me):
    denominators = jnp.concatenate([sums, jnp.ones((124, 128), F32)], axis=0).T
    wide = jnp.concatenate([sums, jnp.ones((12, 128), F32)], axis=0)
    own = jnp.sum(jnp.where(iota((16, 128), 1) == me, wide, 0.0), axis=1, keepdims=True)
    below = []
    for j in range(CAP):
        of = case[j * DEVICES : (j + 1) * DEVICES]
        below.append(
            jnp.where(
                of == 0.0,
                denominators[:, 0:1],
                jnp.where(of == 1.0, denominators[:, 1:2], denominators[:, 2:3]),
            )
        )
    below = jnp.concatenate(below + [own], axis=0)
    is_case = jnp.where(iota((MEMBERS, 1), 0) >= SLOTS, 1.0, 0.0)
    return jnp.where(taken > 0.0, weight * (raised / below - is_case), 0.0)


def kernel(
    history_in,
    qkv_in,
    out_in,
    pool_in,
    head_in,
    table_in,
    risk_ref,
    control_ref,
    case_rows,
    buckets,
    case_weight,
    grad_input_out,
    qkv_out,
    out_out,
    pool_out,
    head_out,
    history,
    qkv_weight,
    out_weight,
    pool_weight,
    head_weight,
    table,
    normed,
    inverse,
    packed,
    attention,
    mixture,
    residual_low,
    slope,
    pooled,
    hidden,
    head_slope,
    grad_preact,
    grad_residual,
    grad_packed,
    normed_t,
    mixture_t,
    residual_t,
    hidden_t,
    facts,
    facts_in,
    facts_mine,
    sums_own,
    sums_middle,
    sums_row,
    sums_col,
    load_sem,
    store_sem,
    fact_col_send,
    fact_col_recv,
    fact_row_send,
    fact_row_recv,
    sum_row_send,
    sum_row_recv,
    sum_col_send,
    sum_col_recv,
    swap_send,
    swap_recv,
    first_send,
    first_recv,
    second_send,
    second_recv,
    third_send,
    third_recv,
    *buffers,
):
    part, swap, first, second_sum, second, third_sum, third = (
        buffers[i * COUNT : (i + 1) * COUNT] for i in range(7)
    )
    grad_pre, grad_residual_low, grad_mixture = residual_low, normed, mixture
    row = lax.axis_index("rows")
    col = lax.axis_index("cols")
    here = {"z": lax.div(row, 4), "y": lax.rem(row, 4), "x": lax.div(col, 2), "core": lax.rem(col, 2)}
    core = here["core"]
    twin = device_at({**here, "core": 1 - core})
    me = row * 8 + col
    row_peers = [(lax.rem(row + step, 16), col) for step in range(1, 16)]
    col_peers = [(row, lax.rem(col + step, 8)) for step in range(1, 8)]
    sends = []

    def send(copy):
        copy.start()
        sends.append(copy)

    def arrived(target, sem):
        remote(target, target, sem, sem, twin).wait_recv()

    loads = [
        pltpu.make_async_copy(source, target, load_sem.at[i])
        for i, (source, target) in enumerate(
            (
                (history_in, history),
                (qkv_in.at[:, 0:D], qkv_weight.at[:, 0:D]),
                (qkv_in.at[:, D : 2 * D], qkv_weight.at[:, D : 2 * D]),
                (qkv_in.at[:, 2 * D : 3 * D], qkv_weight.at[:, 2 * D : 3 * D]),
                (out_in, out_weight),
                (pool_in, pool_weight),
                (head_in, head_weight),
                (table_in, table),
            )
        )
    ]
    for copy in loads:
        copy.start()
    barrier = pltpu.get_barrier_semaphore()
    for peer in row_peers + col_peers:
        pl.semaphore_signal(barrier, inc=1, device_id=peer, device_id_type=MESH)
    lane = iota((1, 128), 1)
    controls = control_ref[...].astype(F32)
    mine = jnp.concatenate(
        [controls[c : c + 1] for c in range(C_DEV)] + [jnp.zeros((1, 128 - C_DEV * K), F32)], axis=1
    )
    wide_lane, wide_row = iota((16, 128), 1), iota((16, 128), 0)
    own = jnp.where((wide_lane == 3) & (wide_row < C_DEV), 1.0, 0.0)
    for c in range(C_DEV):
        bucket, weight = buckets[c].astype(F32), case_weight[c]
        mine = jnp.where(lane == 96 + c, bucket, mine)
        mine = jnp.where(lane == 99 + c, weight, mine)
        for place, value in enumerate((case_rows[c].astype(F32), bucket, weight)):
            own = jnp.where((wide_lane == place) & (wide_row == c), value, own)
    facts_mine[...] = jnp.broadcast_to(mine, (8, 128))

    loads[0].wait()

    def normalise(r):
        rows = block(r, S)
        x = history[rows, :].astype(F32)
        inv = lax.rsqrt(jnp.mean(x * x, axis=1, keepdims=True) + 1e-05)
        inverse[rows, :] = inv
        normed[rows, :] = (x * inv).astype(BF16)

    loop(R_DEV, normalise)
    pl.semaphore_wait(barrier, len(row_peers) + len(col_peers))
    for i, peer in enumerate(col_peers):
        send(
            remote(facts_mine, facts_in.at[i], fact_col_send.at[i], fact_col_recv.at[i], peer)
        )
    for n in range(3):
        loads[1 + n].wait()
        cols = slice(n * D, (n + 1) * D)
        packed[:, cols] = dot(normed[...], qkv_weight[:, cols]).astype(BF16)

    sub = iota((8, 128), 0)
    tile = jnp.where(sub == col, facts_mine[...], 0.0)
    for i in range(7):
        arrived(facts_in.at[i], fact_col_recv.at[i])
        tile = jnp.where(sub == lax.rem(col + 7 - i, 8), facts_in[i], tile)
    facts[row] = tile
    for i, peer in enumerate(row_peers):
        send(
            remote(facts.at[row], facts.at[row], fact_row_send.at[i], fact_row_recv.at[i], peer)
        )

    low_half = iota((S, 128), 1) < HD

    def halves(values):
        zero = jnp.zeros_like(values)
        return jnp.concatenate(
            [jnp.where(low_half, values, zero), jnp.where(low_half, zero, values)], axis=0
        )

    def joined(values):
        return jnp.where(low_half, values[:S], values[S:])

    def attend(r):
        rows = block(r, S)
        for p in range(PAIRS):
            query = packed[rows, p * 128 : p * 128 + 128]
            key = packed[rows, D + p * 128 : D + p * 128 + 128]
            value = packed[rows, 2 * D + p * 128 : 2 * D + p * 128 + 128]
            raised = jnp.exp(dot(halves(key), query, 1, 1) * (1.0 / math.sqrt(HD)))
            low = jnp.concatenate(
                [
                    raised[:S] * (1.0 / jnp.sum(raised[:S], axis=0, keepdims=True)),
                    raised[S:] * (1.0 / jnp.sum(raised[S:], axis=0, keepdims=True)),
                ],
                axis=0,
            ).astype(BF16)
            attention[r, p] = low
            mixture[rows, p * 128 : p * 128 + 128] = dot(low, halves(value), 0, 0).astype(BF16)

    loop(R_DEV, attend)
    loads[4].wait()

    def add_residual(n):
        cols = block(n, 512)
        residual = history[:, cols].astype(F32) + dot(mixture[...], out_weight[:, cols])
        residual_low[:, cols] = residual.astype(BF16)

    loop(2, add_residual)
    loads[5].wait()
    sub16 = iota((16, 512), 0)

    def pool(n):
        cols = block(n, 512)
        active = jnp.tanh(dot(residual_low[...], pool_weight[:, cols]))
        slope[:, cols] = (1.0 - active * active) * (1.0 / math.sqrt(S))
        rows = jnp.zeros((16, 512), F32)
        for r in range(R_DEV):
            total = jnp.sum(active[r * S : (r + 1) * S], axis=0, keepdims=True)
            rows = jnp.where(sub16 == r, total * (1.0 / math.sqrt(S)), rows)
        pooled[:, cols] = rows.astype(BF16).astype(F32)

    loop(2, pool)

    for i in range(15):
        source = lax.rem(row + 15 - i, 16)
        arrived(facts.at[source], fact_row_recv.at[i])
    at_row, case, bucket, weight, taken = find_slots(facts[...].reshape(DEVICES, 128), own, me)
    loads[6].wait()
    loads[7].wait()
    onehot = jnp.where(iota((MEMBERS, NB), 1).astype(F32) == bucket, 1.0, 0.0).astype(BF16)
    onehots = jnp.concatenate([onehot] * 3, axis=1)

    def embed(n):
        cols = block(n, 512)
        times = table[:, cols]
        high = times.astype(BF16)
        middle = (times - high.astype(F32)).astype(BF16)
        low = (times - high.astype(F32) - middle.astype(F32)).astype(BF16)
        rows = pooled[:, cols]
        picked = jnp.where(at_row == 0.0, rows[0:1], jnp.where(at_row == 1.0, rows[1:2], rows[2:3]))
        hidden[:, cols] = (
            picked + dot(onehots, jnp.concatenate([high, middle, low], axis=0))
        ).astype(BF16)

    loop(2, embed)

    def score(n, total):
        cols = block(n, 512)
        preact = dot(hidden[...], head_weight[:, cols])
        gated = jax.nn.sigmoid(preact)
        risk = risk_ref[:, cols]
        head_slope[:, cols] = risk * gated * (1.0 + preact * (1.0 - gated))
        return total + jnp.sum(preact * gated * risk, axis=1, keepdims=True)

    raised = jnp.exp(lax.fori_loop(0, 2, score, jnp.zeros((MEMBERS, 1), F32)))

    sums = partial_sums(raised, case, taken, me)
    sums_own[...] = sums
    for i, peer in enumerate(row_peers):
        send(remote(sums_own, sums_row.at[i], sum_row_send.at[i], sum_row_recv.at[i], peer))
    normed_t[...] = normed[...].T
    mixture_t[...] = mixture[...].T
    for i in range(15):
        arrived(sums_row.at[i], sum_row_recv.at[i])
        sums = sums + sums_row[i]
    sums_middle[...] = sums
    for i, peer in enumerate(col_peers):
        send(remote(sums_middle, sums_col.at[i], sum_col_send.at[i], sum_col_recv.at[i], peer))
    residual_t[...] = residual_low[...].T
    hidden_t[...] = hidden[...].T
    for i in range(7):
        arrived(sums_col.at[i], sum_col_recv.at[i])
        sums = sums + sums_col[i]

    grad_risk = risk_grads(sums, case, weight, taken, raised, me)
    row_of = jnp.where(
        (iota((MEMBERS, 128), 1).astype(F32) == at_row) & (taken > 0.0), 1.0, 0.0
    ).astype(BF16)

    def score_grad(n):
        cols = block(n, 512)
        grad = (grad_risk * head_slope[:, cols]).astype(BF16)
        grad_preact[:, cols] = grad
        pooled[:, cols] = dot(row_of, grad, 0, 0)[0:16]

    loop(2, score_grad)
    sides = {
        "head": (hidden_t, 1, grad_preact, head_out),
        "pool": (residual_t, 1, grad_pre, pool_out),
        "out": (mixture_t, 1, grad_residual_low, out_out),
        "qkv": (normed_t, 1, grad_packed, qkv_out),
    }

    def produce(g):
        width, order = GROUPS[g][2:]
        results = []
        for name, col0 in GROUPS[g][:2]:
            lhs, contract, rhs, _ = sides[name]
            grad = dot(lhs[...], rhs[:, col0 : col0 + width], contract, 0)
            results.append(grad.reshape(4, 4, 4, 2, 8, width))
        for c in range(2):
            for z in range(4):
                for y in range(4):
                    values = jnp.concatenate(
                        [result[z, y, :, c] for result in results], axis=1
                    ).astype(BF16)
                    if order == "zyx":
                        part[g][c, z, y] = values
                    elif order == "yxz":
                        part[g][c, y, :, z] = values
                    else:
                        part[g][c, :, z, y] = values
        send(remote(part[g].at[1 - core], swap[g], swap_send.at[g], swap_recv.at[g], twin))

    def ring(g):
        at = here[GROUPS[g][3][0]]
        return at, lax.rem(at + 1, 4), lax.rem(at + 2, 4), lax.rem(at + 3, 4)

    def send_first(g, slot, digit, half, step):
        send(
            remote(
                part[g].at[core, digit, pl.ds(half, 2)],
                first[g].at[slot],
                first_send.at[g, slot],
                first_recv.at[g, slot],
                device_at(moved(here, GROUPS[g][3][0], step)),
            )
        )

    def first_spread(g):
        at, right, far, left = ring(g)
        arrived(swap[g], swap_recv.at[g])
        for b in range(4):
            part[g][core, far, b] = added(part[g][core, far, b], swap[g][far, b]).astype(BF16)
        send_first(g, 0, far, 0, 1)
        send_first(g, 1, far, 2, 3)
        for b in range(2):
            part[g][core, right, 2 + b] = added(
                part[g][core, right, 2 + b], swap[g][right, 2 + b]
            ).astype(BF16)
            part[g][core, left, b] = added(part[g][core, left, b], swap[g][left, b]).astype(BF16)
        send_first(g, 2, right, 2, 1)
        send_first(g, 3, left, 0, 3)

    def first_relay(g):
        at, right, far, left = ring(g)
        for slot, came, digit, half, step in ((4, 0, right, 0, 1), (5, 1, left, 2, 3)):
            arrived(first[g].at[came], first_recv.at[g, came])
            for k in range(2):
                b = half + k
                part[g][core, digit, b] = added(
                    part[g][core, digit, b], swap[g][digit, b], first[g][came, k]
                ).astype(BF16)
            send_first(g, slot, digit, half, step)

    def second_spread(g):
        at = ring(g)[0]
        for slot in (2, 3, 4, 5):
            arrived(first[g].at[slot], first_recv.at[g, slot])
        for b in range(4):
            one, other = (3, 4) if b < 2 else (2, 5)
            second_sum[g][b] = added(
                part[g][core, at, b], swap[g][at, b], first[g][one, b % 2], first[g][other, b % 2]
            ).astype(BF16)
        direct(GROUPS[g][3][1], second_sum[g], second[g], second_send.at[g], second_recv.at[g])

    def direct(axis, source, landing, send_sems, recv_sems):
        for step in (2, 1, 3):
            send(
                remote(
                    source.at[lax.rem(here[axis] + step, 4)],
                    landing.at[step - 1],
                    send_sems.at[step - 1],
                    recv_sems.at[step - 1],
                    device_at(moved(here, axis, step)),
                )
            )

    def third_spread(g):
        at = here[GROUPS[g][3][1]]
        for slot in range(3):
            arrived(second[g].at[slot], second_recv.at[g, slot])
        third_sum[g][...] = added(second_sum[g][at], second[g][0], second[g][1], second[g][2]).astype(
            BF16
        )
        direct(GROUPS[g][3][2], third_sum[g], third[g], third_send.at[g], third_recv.at[g])

    def finish(g):
        width, order = GROUPS[g][2:]
        for slot in range(3):
            arrived(third[g].at[slot], third_recv.at[g, slot])
        total = added(third_sum[g][here[order[2]]], third[g][0], third[g][1], third[g][2])
        for t, (name, col0) in enumerate(GROUPS[g][:2]):
            sides[name][3][:, col0 : col0 + width] = total[8 * t : 8 * t + 8]

    def back_pooled():
        by_row = pooled[...]
        high = by_row.astype(BF16)
        low = (by_row - high.astype(F32)).astype(BF16)
        by_row = jnp.concatenate([high, low], axis=0)

        def pool_grad(n):
            both = dot(by_row, head_weight[block(n, 512), :], 1, 1)
            grad = both[0:16] + both[16:32]
            cols = block(n, 512)
            for r in range(R_DEV):
                rows = slice(r * S, (r + 1) * S)
                grad_pre[rows, cols] = (grad[r : r + 1] * slope[rows, cols]).astype(BF16)

        loop(2, pool_grad)

    def back_residual():
        def step(n):
            cols = block(n, 512)
            grad = dot(grad_pre[...], pool_weight[cols, :], 1, 1)
            grad_residual[:, cols] = grad
            grad_residual_low[:, cols] = grad.astype(BF16)

        loop(2, step)

    def back_mixture():
        def step(n):
            cols = block(n, 512)
            grad_mixture[:, cols] = dot(grad_residual_low[...], out_weight[cols, :], 1, 1).astype(BF16)

        loop(2, step)

    def back_attend_one(r, p):
        rows = slice(r * S, (r + 1) * S)
        query_at, key_at, value_at = (slice(i * D + p * 128, i * D + p * 128 + 128) for i in range(3))
        query, key, value = packed[rows, query_at], packed[rows, key_at], packed[rows, value_at]
        grad = grad_mixture[rows, query_at]
        low = attention[r, p]
        weights = low.astype(F32)
        grad_attention = dot(halves(value), grad, 1, 1)
        product = weights * grad_attention
        scale = 1.0 / math.sqrt(HD)
        grad_logits = jnp.concatenate(
            [
                weights[at]
                * (grad_attention[at] - jnp.sum(product[at], axis=0, keepdims=True))
                * scale
                for at in (slice(0, S), slice(S, 2 * S))
            ],
            axis=0,
        ).astype(BF16)
        grad_packed[rows, query_at] = dot(grad_logits, halves(key), 0, 0).astype(BF16)
        grad_packed[rows, key_at] = joined(dot(grad_logits, query)).astype(BF16)
        grad_packed[rows, value_at] = joined(dot(low, grad)).astype(BF16)

    def back_attend(first_pair, pairs):
        for r in range(R_DEV):
            for p in range(first_pair, first_pair + pairs):
                back_attend_one(r, p)

    def back_normed(n):
        cols = slice(n * 512, (n + 1) * 512)
        head_slope[0:TOKENS, cols] = dot(grad_packed[...], qkv_weight[cols, :], 1, 1)

    stores = []

    def back_input():
        for r in range(R_DEV):
            rows = slice(r * S, (r + 1) * S)
            grad = head_slope[rows, :]
            x = history[rows, :].astype(F32)
            inv = inverse[rows, :]
            mean = jnp.mean(grad * x, axis=1, keepdims=True)
            head_slope[rows, :] = grad_residual[rows, :] + inv * grad - x * (inv * inv * inv * mean)
            stores.append(
                pltpu.make_async_copy(head_slope.at[rows], grad_input_out.at[rows], store_sem.at[r])
            )
            stores[-1].start()

    a, b, c, d, e, f = produce, first_spread, first_relay, second_spread, third_spread, finish
    def drain():
        while sends:
            sends.pop(0).wait_send()

    plan = (
        (a, 0), (back_pooled,), (a, 1), (back_residual,), (b, 0), (a, 2), (b, 1), (back_mixture,), (b, 2),
        (back_attend, 0, 4), (a, 3), (a, 4), (a, 5), (c, 0), (c, 1), (c, 2), (b, 3), (b, 4), (b, 5),
        (back_attend, 4, 4), (a, 6), (a, 7), (a, 8), (d, 0), (d, 1), (c, 3), (c, 4), (b, 6), (b, 7),
        (b, 8), (c, 5), (d, 2), (e, 0), (e, 1), (c, 6), (c, 7), (c, 8), (back_normed, 0), (d, 3), (d, 4),
        (d, 5), (e, 2), (d, 6), (d, 7), (d, 8), (back_normed, 1), (e, 3), (e, 4), (e, 5), (e, 6), (e, 7),
        (e, 8), (back_input,), (f, 0), (f, 1), (f, 2), (drain,), (f, 3), (f, 4), (f, 5), (f, 6), (f, 7),
        (f, 8),
    )
    for stage, *at in plan:
        stage(*at)

    drain()
    for copy in stores:
        copy.wait()


def deliver(results):
    steps = 2

    def copy_kernel(*refs):
        for source, target in zip(refs[: len(results)], refs[len(results) :]):
            target[...] = source[...]

    specs = [pl.BlockSpec((TOKENS // steps, D), lambda i: (i, 0))]
    for result in results[1:]:
        specs.append(pl.BlockSpec((8, result.shape[1] // steps), lambda i: (0, i)))
    return pl.pallas_call(
        copy_kernel,
        grid=(steps,),
        out_shape=tuple(jax.ShapeDtypeStruct(x.shape, x.dtype) for x in results),
        in_specs=specs,
        out_specs=tuple(specs),
    )(*results)


def body(
    history,
    qkv_weight,
    out_weight,
    pool_weight,
    head_weight,
    risk_weight,
    time_table,
    case_rows,
    control_rows,
    buckets,
    case_weight,
):
    vmem = pl.BlockSpec(memory_space=pltpu.VMEM)
    smem = pl.BlockSpec(memory_space=pltpu.SMEM)
    hbm = pl.BlockSpec(memory_space=pl.ANY)
    dma = pltpu.SemaphoreType.DMA
    results = pl.pallas_call(
        kernel,
        out_shape=(
            jax.ShapeDtypeStruct((TOKENS, D), F32),
            jax.ShapeDtypeStruct((8, 3 * D), F32),
            jax.ShapeDtypeStruct((8, D), F32),
            jax.ShapeDtypeStruct((8, D), F32),
            jax.ShapeDtypeStruct((8, D), F32),
        ),
        in_specs=[hbm] * 6 + [vmem] * 2 + [smem] * 3,
        out_specs=(hbm,) + (vmem,) * 4,
        scratch_shapes=[
            pltpu.VMEM((TOKENS, D), BF16),
            pltpu.VMEM((D, 3 * D), BF16),
            pltpu.VMEM((D, D), BF16),
            pltpu.VMEM((D, D), BF16),
            pltpu.VMEM((D, D), BF16),
            pltpu.VMEM((NB, D), F32),
            pltpu.VMEM((TOKENS, D), BF16),
            pltpu.VMEM((TOKENS, 1), F32),
            pltpu.VMEM((TOKENS, 3 * D), BF16),
            pltpu.VMEM((R_DEV, PAIRS, 2 * S, S), BF16),
            pltpu.VMEM((TOKENS, D), BF16),
            pltpu.VMEM((TOKENS, D), BF16),
            pltpu.VMEM((TOKENS, D), F32),
            pltpu.VMEM((16, D), F32),
            pltpu.VMEM((MEMBERS, D), BF16),
            pltpu.VMEM((MEMBERS, D), F32),
            pltpu.VMEM((MEMBERS, D), BF16),
            pltpu.VMEM((TOKENS, D), F32),
            pltpu.VMEM((TOKENS, 3 * D), BF16),
            pltpu.VMEM((D, TOKENS), BF16),
            pltpu.VMEM((D, TOKENS), BF16),
            pltpu.VMEM((D, TOKENS), BF16),
            pltpu.VMEM((D, MEMBERS), BF16),
            pltpu.VMEM((16, 8, 128), F32),
            pltpu.VMEM((7, 8, 128), F32),
            pltpu.VMEM((8, 128), F32),
            pltpu.VMEM((4, 128), F32),
            pltpu.VMEM((4, 128), F32),
            pltpu.VMEM((15, 4, 128), F32),
            pltpu.VMEM((7, 4, 128), F32),
            dma((8,)),
            dma((3,)),
            dma((7,)),
            dma((7,)),
            dma((15,)),
            dma((15,)),
            dma((15,)),
            dma((15,)),
            dma((7,)),
            dma((7,)),
            dma((COUNT,)),
            dma((COUNT,)),
            dma((COUNT, 6)),
            dma((COUNT, 6)),
            dma((COUNT, 3)),
            dma((COUNT, 3)),
            dma((COUNT, 3)),
            dma((COUNT, 3)),
        ]
        + [
            pltpu.VMEM((*shape, 16, group[2]), BF16)
            for shape in (
                (2, 4, 4, 4),
                (4, 4, 4),
                (6, 2, 4),
                (4, 4),
                (3, 4),
                (4,),
                (3,),
            )
            for group in GROUPS
        ],
        compiler_params=pltpu.CompilerParams(
            collective_id=1, has_side_effects=True, vmem_limit_bytes=62 * 2**20
        ),
    )(
        history.reshape(TOKENS, D),
        qkv_weight,
        out_weight,
        pool_weight,
        head_weight,
        time_table,
        risk_weight[None],
        control_rows,
        case_rows,
        buckets,
        case_weight,
    )
    grad_input, *shares = deliver(results)
    return (grad_input.reshape(R_DEV, S, D), *shares)


def solution(mesh):
    in_specs = (
        P(("rows", "cols"), None, None),
        P(),
        P(),
        P(),
        P(),
        P(),
        P(),
        P(("rows", "cols")),
        P(("rows", "cols"), None),
        P(("rows", "cols")),
        P(("rows", "cols")),
    )
    out_specs = (
        P(("rows", "cols"), None, None),
        P(("rows", "cols"), None),
        P(("rows", "cols"), None),
        P(("rows", "cols"), None),
        P(("rows", "cols"), None),
    )
    return jax.shard_map(body, mesh=mesh, in_specs=in_specs, out_specs=out_specs, check_vma=False)
```

```python
import math

import jax
import jax.numpy as jnp
from jax import lax
from jax.experimental import pallas as pl
from jax.experimental.pallas import tpu as pltpu
from jax.sharding import PartitionSpec as P

D = 1024
HD = 64
HEADS = 16
S = 128
K = 32
CAP = 4
NB = 128
R_DEV = 3
C_DEV = 3
TOKENS = R_DEV * S
DEVICES = 128
SLOTS = CAP * DEVICES
MEMBERS = SLOTS + 16
PAIRS = HEADS // 2

MESH = pl.DeviceIdType.MESH
F32 = jnp.float32
BF16 = jnp.bfloat16

GROUPS = (
    (("head", 0), ("head", 512), 512, "zyx"),
    (("pool", 0), ("pool", 512), 512, "yxz"),
    (("out", 0), ("out", 512), 512, "xzy"),
    (("qkv", 0), ("qkv", D), 256, "zyx"),
    (("qkv", 256), ("qkv", D + 256), 256, "yxz"),
    (("qkv", 2 * D), ("qkv", 2 * D + 256), 256, "xzy"),
    (("qkv", 512), ("qkv", D + 512), 256, "zyx"),
    (("qkv", 768), ("qkv", D + 768), 256, "yxz"),
    (("qkv", 2 * D + 512), ("qkv", 2 * D + 768), 256, "xzy"),
)
COUNT = len(GROUPS)


def device_at(place):
    return (place["z"] * 4 + place["y"], place["x"] * 2 + place["core"])


def moved(place, axis, step):
    return {**place, axis: lax.rem(place[axis] + step, 4)}


def remote(source, target, send_sem, recv_sem, device):
    return pltpu.make_async_remote_copy(
        src_ref=source,
        dst_ref=target,
        send_sem=send_sem,
        recv_sem=recv_sem,
        device_id=device,
        device_id_type=MESH,
    )


def added(*parts):
    total = parts[0].astype(F32)
    for part in parts[1:]:
        total = total + part.astype(F32)
    return total


def iota(shape, dim):
    return lax.broadcasted_iota(jnp.int32, shape, dim)


def dot(a, b, contract_a=1, contract_b=0):
    return lax.dot_general(
        a, b, (((contract_a,), (contract_b,)), ((), ())), preferred_element_type=F32
    )


def block(i, size):
    return pl.ds(pl.multiple_of(i * size, size), size)


def loop(count, step, unroll=1):
    def run(i, carry):
        step(i)
        return carry

    lax.fori_loop(0, count, run, 0, unroll=unroll)


def find_slots(facts, own, me):
    lane = iota((DEVICES, 128), 1)
    local = facts - (R_DEV * me).astype(F32)
    hit = (lane < C_DEV * K) & (local >= 0.0) & (local < float(R_DEV))
    hits = jnp.where(hit, 1.0, 0.0)
    before = jnp.where(iota((128, 128), 0) < iota((128, 128), 1), 1.0, 0.0).astype(BF16)
    order = dot(hits.astype(BF16), before)
    case_of = jnp.where(lane < K, 0.0, jnp.where(lane < 2 * K, 1.0, 2.0))
    columns = [[], [], [], [], []]
    for j in range(CAP):
        chosen = jnp.where(order == float(j), hits, 0.0)
        row = jnp.sum(chosen * local, axis=1, keepdims=True)
        case = jnp.sum(chosen * case_of, axis=1, keepdims=True)
        taken = jnp.sum(chosen, axis=1, keepdims=True)
        bucket = jnp.zeros_like(row)
        weight = jnp.zeros_like(row)
        for c in range(C_DEV):
            is_c = case == float(c)
            bucket = jnp.where(is_c, facts[:, 96 + c : 97 + c], bucket)
            weight = jnp.where(is_c, facts[:, 99 + c : 100 + c], weight)
        for column, values in zip(columns, (row, case, bucket, weight, taken)):
            column.append(values)
    own_case = iota((16, 1), 0).astype(F32)
    for column, values in zip(
        columns, (own[:, 0:1], own_case, own[:, 1:2], own[:, 2:3], own[:, 3:4])
    ):
        column.append(values)
    return [jnp.concatenate(column, axis=0) for column in columns]


def partial_sums(raised, case, taken, me):
    raised = jnp.where(taken > 0.0, raised, 0.0)
    lane = iota((DEVICES, 128), 1)
    mine = iota((DEVICES, 128), 0) == me
    sums = jnp.zeros((DEVICES, 128), F32)
    for c in range(C_DEV):
        share = jnp.zeros((DEVICES, 1), F32)
        for j in range(CAP):
            at = slice(j * DEVICES, (j + 1) * DEVICES)
            share = share + jnp.where(case[at] == float(c), raised[at], 0.0)
        share = share + jnp.where(mine, raised[SLOTS + c : SLOTS + c + 1], 0.0)
        sums = jnp.where(lane == c, share, sums)
    return sums.T[0:4]


def risk_grads(sums, case, weight, taken, raised, me):
    denominators = jnp.concatenate([sums, jnp.ones((124, 128), F32)], axis=0).T
    wide = jnp.concatenate([sums, jnp.ones((12, 128), F32)], axis=0)
    own = jnp.sum(jnp.where(iota((16, 128), 1) == me, wide, 0.0), axis=1, keepdims=True)
    below = []
    for j in range(CAP):
        of = case[j * DEVICES : (j + 1) * DEVICES]
        below.append(
            jnp.where(
                of == 0.0,
                denominators[:, 0:1],
                jnp.where(of == 1.0, denominators[:, 1:2], denominators[:, 2:3]),
            )
        )
    below = jnp.concatenate(below + [own], axis=0)
    is_case = jnp.where(iota((MEMBERS, 1), 0) >= SLOTS, 1.0, 0.0)
    return jnp.where(taken > 0.0, weight * (raised / below - is_case), 0.0)


def kernel(
    history_in,
    qkv_in,
    out_in,
    pool_in,
    head_in,
    table_in,
    risk_ref,
    control_ref,
    case_rows,
    buckets,
    case_weight,
    grad_input_out,
    qkv_out,
    out_out,
    pool_out,
    head_out,
    history,
    qkv_weight,
    out_weight,
    pool_weight,
    head_weight,
    table,
    normed,
    inverse,
    packed,
    attention,
    mixture,
    residual_low,
    slope,
    pooled,
    hidden,
    head_slope,
    grad_preact,
    grad_residual,
    grad_packed,
    normed_t,
    mixture_t,
    residual_t,
    hidden_t,
    facts,
    facts_in,
    facts_mine,
    sums_own,
    sums_middle,
    sums_row,
    sums_col,
    load_sem,
    store_sem,
    fact_col_send,
    fact_col_recv,
    fact_row_send,
    fact_row_recv,
    sum_row_send,
    sum_row_recv,
    sum_col_send,
    sum_col_recv,
    swap_send,
    swap_recv,
    first_send,
    first_recv,
    second_send,
    second_recv,
    third_send,
    third_recv,
    *buffers,
):
    part, swap, first, second_sum, second, third_sum, third = (
        buffers[i * COUNT : (i + 1) * COUNT] for i in range(7)
    )
    grad_pre, grad_residual_low, grad_mixture = residual_low, normed, mixture
    row = lax.axis_index("rows")
    col = lax.axis_index("cols")
    here = {"z": lax.div(row, 4), "y": lax.rem(row, 4), "x": lax.div(col, 2), "core": lax.rem(col, 2)}
    core = here["core"]
    twin = device_at({**here, "core": 1 - core})
    me = row * 8 + col
    row_peers = [(lax.rem(row + step, 16), col) for step in range(1, 16)]
    col_peers = [(row, lax.rem(col + step, 8)) for step in range(1, 8)]
    sends = []

    def send(copy):
        copy.start()
        sends.append(copy)

    def arrived(target, sem):
        remote(target, target, sem, sem, twin).wait_recv()

    loads = [
        pltpu.make_async_copy(source, target, load_sem.at[i])
        for i, (source, target) in enumerate(
            (
                (history_in, history),
                (qkv_in.at[:, 0:D], qkv_weight.at[:, 0:D]),
                (qkv_in.at[:, D : 2 * D], qkv_weight.at[:, D : 2 * D]),
                (qkv_in.at[:, 2 * D : 3 * D], qkv_weight.at[:, 2 * D : 3 * D]),
                (out_in, out_weight),
                (pool_in, pool_weight),
                (head_in, head_weight),
                (table_in, table),
            )
        )
    ]
    for copy in loads:
        copy.start()
    barrier = pltpu.get_barrier_semaphore()
    for peer in row_peers + col_peers:
        pl.semaphore_signal(barrier, inc=1, device_id=peer, device_id_type=MESH)
    lane = iota((1, 128), 1)
    controls = control_ref[...].astype(F32)
    mine = jnp.concatenate(
        [controls[c : c + 1] for c in range(C_DEV)] + [jnp.zeros((1, 128 - C_DEV * K), F32)], axis=1
    )
    wide_lane, wide_row = iota((16, 128), 1), iota((16, 128), 0)
    own = jnp.where((wide_lane == 3) & (wide_row < C_DEV), 1.0, 0.0)
    for c in range(C_DEV):
        bucket, weight = buckets[c].astype(F32), case_weight[c]
        mine = jnp.where(lane == 96 + c, bucket, mine)
        mine = jnp.where(lane == 99 + c, weight, mine)
        for place, value in enumerate((case_rows[c].astype(F32), bucket, weight)):
            own = jnp.where((wide_lane == place) & (wide_row == c), value, own)
    facts_mine[...] = jnp.broadcast_to(mine, (8, 128))

    loads[0].wait()

    def normalise(r):
        rows = block(r, S)
        x = history[rows, :].astype(F32)
        inv = lax.rsqrt(jnp.mean(x * x, axis=1, keepdims=True) + 1e-05)
        inverse[rows, :] = inv
        normed[rows, :] = (x * inv).astype(BF16)

    loop(R_DEV, normalise, R_DEV)
    pl.semaphore_wait(barrier, len(row_peers) + len(col_peers))
    for i, peer in enumerate(col_peers):
        send(
            remote(facts_mine, facts_in.at[i], fact_col_send.at[i], fact_col_recv.at[i], peer)
        )
    for n in range(3):
        loads[1 + n].wait()
        cols = slice(n * D, (n + 1) * D)
        packed[:, cols] = dot(normed[...], qkv_weight[:, cols]).astype(BF16)

    sub = iota((8, 128), 0)
    tile = jnp.where(sub == col, facts_mine[...], 0.0)
    for i in range(7):
        arrived(facts_in.at[i], fact_col_recv.at[i])
        tile = jnp.where(sub == lax.rem(col + 7 - i, 8), facts_in[i], tile)
    facts[row] = tile
    for i, peer in enumerate(row_peers):
        send(
            remote(facts.at[row], facts.at[row], fact_row_send.at[i], fact_row_recv.at[i], peer)
        )

    low_half = iota((S, 128), 1) < HD

    def halves(values):
        zero = jnp.zeros_like(values)
        return jnp.concatenate(
            [jnp.where(low_half, values, zero), jnp.where(low_half, zero, values)], axis=0
        )

    def joined(values):
        return jnp.where(low_half, values[:S], values[S:])

    def attend(r):
        rows = block(r, S)
        for p in range(PAIRS):
            query = packed[rows, p * 128 : p * 128 + 128]
            key = packed[rows, D + p * 128 : D + p * 128 + 128]
            value = packed[rows, 2 * D + p * 128 : 2 * D + p * 128 + 128]
            raised = jnp.exp(dot(halves(key), query, 1, 1) * (1.0 / math.sqrt(HD)))
            low = jnp.concatenate(
                [
                    raised[:S] * (1.0 / jnp.sum(raised[:S], axis=0, keepdims=True)),
                    raised[S:] * (1.0 / jnp.sum(raised[S:], axis=0, keepdims=True)),
                ],
                axis=0,
            ).astype(BF16)
            attention[r, p] = low
            mixture[rows, p * 128 : p * 128 + 128] = dot(low, halves(value), 0, 0).astype(BF16)

    loop(R_DEV, attend, R_DEV)
    loads[4].wait()

    def add_residual(n):
        cols = block(n, 512)
        residual = history[:, cols].astype(F32) + dot(mixture[...], out_weight[:, cols])
        residual_low[:, cols] = residual.astype(BF16)

    loop(2, add_residual, 2)
    loads[5].wait()
    sub16 = iota((16, 512), 0)

    def pool(n):
        cols = block(n, 512)
        active = jnp.tanh(dot(residual_low[...], pool_weight[:, cols]))
        slope[:, cols] = (1.0 - active * active) * (1.0 / math.sqrt(S))
        rows = jnp.zeros((16, 512), F32)
        for r in range(R_DEV):
            total = jnp.sum(active[r * S : (r + 1) * S], axis=0, keepdims=True)
            rows = jnp.where(sub16 == r, total * (1.0 / math.sqrt(S)), rows)
        pooled[:, cols] = rows.astype(BF16).astype(F32)

    loop(2, pool, 2)

    for i in range(15):
        source = lax.rem(row + 15 - i, 16)
        arrived(facts.at[source], fact_row_recv.at[i])
    at_row, case, bucket, weight, taken = find_slots(facts[...].reshape(DEVICES, 128), own, me)
    loads[6].wait()
    loads[7].wait()
    onehot = jnp.where(iota((MEMBERS, NB), 1).astype(F32) == bucket, 1.0, 0.0).astype(BF16)
    onehots = jnp.concatenate([onehot] * 3, axis=1)

    def embed(n):
        cols = block(n, 512)
        times = table[:, cols]
        high = times.astype(BF16)
        middle = (times - high.astype(F32)).astype(BF16)
        low = (times - high.astype(F32) - middle.astype(F32)).astype(BF16)
        rows = pooled[:, cols]
        picked = jnp.where(at_row == 0.0, rows[0:1], jnp.where(at_row == 1.0, rows[1:2], rows[2:3]))
        hidden[:, cols] = (
            picked + dot(onehots, jnp.concatenate([high, middle, low], axis=0))
        ).astype(BF16)

    loop(2, embed, 2)

    def score(n, total):
        cols = block(n, 512)
        preact = dot(hidden[...], head_weight[:, cols])
        gated = jax.nn.sigmoid(preact)
        risk = risk_ref[:, cols]
        head_slope[:, cols] = risk * gated * (1.0 + preact * (1.0 - gated))
        return total + jnp.sum(preact * gated * risk, axis=1, keepdims=True)

    raised = jnp.exp(lax.fori_loop(0, 2, score, jnp.zeros((MEMBERS, 1), F32), unroll=2))

    sums = partial_sums(raised, case, taken, me)
    sums_own[...] = sums
    for i, peer in enumerate(row_peers):
        send(remote(sums_own, sums_row.at[i], sum_row_send.at[i], sum_row_recv.at[i], peer))
    normed_t[...] = normed[...].T
    mixture_t[...] = mixture[...].T
    for i in range(15):
        arrived(sums_row.at[i], sum_row_recv.at[i])
        sums = sums + sums_row[i]
    sums_middle[...] = sums
    for i, peer in enumerate(col_peers):
        send(remote(sums_middle, sums_col.at[i], sum_col_send.at[i], sum_col_recv.at[i], peer))
    residual_t[...] = residual_low[...].T
    hidden_t[...] = hidden[...].T
    for i in range(7):
        arrived(sums_col.at[i], sum_col_recv.at[i])
        sums = sums + sums_col[i]

    grad_risk = risk_grads(sums, case, weight, taken, raised, me)
    row_of = jnp.where(
        (iota((MEMBERS, 128), 1).astype(F32) == at_row) & (taken > 0.0), 1.0, 0.0
    ).astype(BF16)

    def score_grad(n):
        cols = block(n, 512)
        grad = (grad_risk * head_slope[:, cols]).astype(BF16)
        grad_preact[:, cols] = grad
        pooled[:, cols] = dot(row_of, grad, 0, 0)[0:16]

    loop(2, score_grad, 2)
    sides = {
        "head": (hidden_t, 1, grad_preact, head_out),
        "pool": (residual_t, 1, grad_pre, pool_out),
        "out": (mixture_t, 1, grad_residual_low, out_out),
        "qkv": (normed_t, 1, grad_packed, qkv_out),
    }

    def produce(g):
        width, order = GROUPS[g][2:]
        results = []
        for name, col0 in GROUPS[g][:2]:
            lhs, contract, rhs, _ = sides[name]
            grad = dot(lhs[...], rhs[:, col0 : col0 + width], contract, 0)
            results.append(grad.reshape(4, 4, 4, 2, 8, width))
        for c in range(2):
            for z in range(4):
                for y in range(4):
                    values = jnp.concatenate(
                        [result[z, y, :, c] for result in results], axis=1
                    ).astype(BF16)
                    if order == "zyx":
                        part[g][c, z, y] = values
                    elif order == "yxz":
                        part[g][c, y, :, z] = values
                    else:
                        part[g][c, :, z, y] = values
        send(remote(part[g].at[1 - core], swap[g], swap_send.at[g], swap_recv.at[g], twin))

    def ring(g):
        at = here[GROUPS[g][3][0]]
        return at, lax.rem(at + 1, 4), lax.rem(at + 2, 4), lax.rem(at + 3, 4)

    def send_first(g, slot, digit, half, step):
        send(
            remote(
                part[g].at[core, digit, pl.ds(half, 2)],
                first[g].at[slot],
                first_send.at[g, slot],
                first_recv.at[g, slot],
                device_at(moved(here, GROUPS[g][3][0], step)),
            )
        )

    def first_spread(g):
        at, right, far, left = ring(g)
        arrived(swap[g], swap_recv.at[g])
        for b in range(4):
            part[g][core, far, b] = added(part[g][core, far, b], swap[g][far, b]).astype(BF16)
        send_first(g, 0, far, 0, 1)
        send_first(g, 1, far, 2, 3)
        for b in range(2):
            part[g][core, right, 2 + b] = added(
                part[g][core, right, 2 + b], swap[g][right, 2 + b]
            ).astype(BF16)
            part[g][core, left, b] = added(part[g][core, left, b], swap[g][left, b]).astype(BF16)
        send_first(g, 2, right, 2, 1)
        send_first(g, 3, left, 0, 3)

    def first_relay(g):
        at, right, far, left = ring(g)
        for slot, came, digit, half, step in ((4, 0, right, 0, 1), (5, 1, left, 2, 3)):
            arrived(first[g].at[came], first_recv.at[g, came])
            for k in range(2):
                b = half + k
                part[g][core, digit, b] = added(
                    part[g][core, digit, b], swap[g][digit, b], first[g][came, k]
                ).astype(BF16)
            send_first(g, slot, digit, half, step)

    def second_spread(g):
        at = ring(g)[0]
        for slot in (2, 3, 4, 5):
            arrived(first[g].at[slot], first_recv.at[g, slot])
        for b in range(4):
            one, other = (3, 4) if b < 2 else (2, 5)
            second_sum[g][b] = added(
                part[g][core, at, b], swap[g][at, b], first[g][one, b % 2], first[g][other, b % 2]
            ).astype(BF16)
        direct(GROUPS[g][3][1], second_sum[g], second[g], second_send.at[g], second_recv.at[g])

    def direct(axis, source, landing, send_sems, recv_sems):
        for step in (2, 1, 3):
            send(
                remote(
                    source.at[lax.rem(here[axis] + step, 4)],
                    landing.at[step - 1],
                    send_sems.at[step - 1],
                    recv_sems.at[step - 1],
                    device_at(moved(here, axis, step)),
                )
            )

    def third_spread(g):
        at = here[GROUPS[g][3][1]]
        for slot in range(3):
            arrived(second[g].at[slot], second_recv.at[g, slot])
        third_sum[g][...] = added(second_sum[g][at], second[g][0], second[g][1], second[g][2]).astype(
            BF16
        )
        direct(GROUPS[g][3][2], third_sum[g], third[g], third_send.at[g], third_recv.at[g])

    def finish(g):
        width, order = GROUPS[g][2:]
        for slot in range(3):
            arrived(third[g].at[slot], third_recv.at[g, slot])
        total = added(third_sum[g][here[order[2]]], third[g][0], third[g][1], third[g][2])
        for t, (name, col0) in enumerate(GROUPS[g][:2]):
            sides[name][3][:, col0 : col0 + width] = total[8 * t : 8 * t + 8]

    def back_pooled():
        by_row = pooled[...]
        high = by_row.astype(BF16)
        low = (by_row - high.astype(F32)).astype(BF16)
        by_row = jnp.concatenate([high, low], axis=0)

        def pool_grad(n):
            both = dot(by_row, head_weight[block(n, 512), :], 1, 1)
            grad = both[0:16] + both[16:32]
            cols = block(n, 512)
            for r in range(R_DEV):
                rows = slice(r * S, (r + 1) * S)
                grad_pre[rows, cols] = (grad[r : r + 1] * slope[rows, cols]).astype(BF16)

        loop(2, pool_grad, 2)

    def back_residual():
        def step(n):
            cols = block(n, 512)
            grad = dot(grad_pre[...], pool_weight[cols, :], 1, 1)
            grad_residual[:, cols] = grad
            grad_residual_low[:, cols] = grad.astype(BF16)

        loop(2, step, 2)

    def back_mixture():
        def step(n):
            cols = block(n, 512)
            grad_mixture[:, cols] = dot(grad_residual_low[...], out_weight[cols, :], 1, 1).astype(BF16)

        loop(2, step, 2)

    def back_attend_one(r, p):
        rows = slice(r * S, (r + 1) * S)
        query_at, key_at, value_at = (slice(i * D + p * 128, i * D + p * 128 + 128) for i in range(3))
        query, key, value = packed[rows, query_at], packed[rows, key_at], packed[rows, value_at]
        grad = grad_mixture[rows, query_at]
        low = attention[r, p]
        weights = low.astype(F32)
        grad_attention = dot(halves(value), grad, 1, 1)
        product = weights * grad_attention
        scale = 1.0 / math.sqrt(HD)
        grad_logits = jnp.concatenate(
            [
                weights[at]
                * (grad_attention[at] - jnp.sum(product[at], axis=0, keepdims=True))
                * scale
                for at in (slice(0, S), slice(S, 2 * S))
            ],
            axis=0,
        ).astype(BF16)
        grad_packed[rows, query_at] = dot(grad_logits, halves(key), 0, 0).astype(BF16)
        grad_packed[rows, key_at] = joined(dot(grad_logits, query)).astype(BF16)
        grad_packed[rows, value_at] = joined(dot(low, grad)).astype(BF16)

    def back_attend(first_pair, pairs):
        for r in range(R_DEV):
            for p in range(first_pair, first_pair + pairs):
                back_attend_one(r, p)

    def back_normed(n):
        cols = slice(n * 512, (n + 1) * 512)
        head_slope[0:TOKENS, cols] = dot(grad_packed[...], qkv_weight[cols, :], 1, 1)

    stores = []

    def back_input():
        for r in range(R_DEV):
            rows = slice(r * S, (r + 1) * S)
            grad = head_slope[rows, :]
            x = history[rows, :].astype(F32)
            inv = inverse[rows, :]
            mean = jnp.mean(grad * x, axis=1, keepdims=True)
            head_slope[rows, :] = grad_residual[rows, :] + inv * grad - x * (inv * inv * inv * mean)
            stores.append(
                pltpu.make_async_copy(head_slope.at[rows], grad_input_out.at[rows], store_sem.at[r])
            )
            stores[-1].start()

    a, b, c, d, e, f = produce, first_spread, first_relay, second_spread, third_spread, finish
    def drain():
        while sends:
            sends.pop(0).wait_send()

    plan = (
        (a, 0), (back_pooled,), (a, 1), (back_residual,), (b, 0), (a, 2), (b, 1), (back_mixture,), (b, 2),
        (back_attend, 0, 4), (a, 3), (a, 4), (a, 5), (c, 0), (c, 1), (c, 2), (b, 3), (b, 4), (b, 5),
        (back_attend, 4, 4), (a, 6), (a, 7), (a, 8), (d, 0), (d, 1), (c, 3), (c, 4), (b, 6), (b, 7),
        (b, 8), (c, 5), (d, 2), (e, 0), (e, 1), (c, 6), (c, 7), (c, 8), (back_normed, 0), (d, 3), (d, 4),
        (d, 5), (e, 2), (d, 6), (d, 7), (d, 8), (back_normed, 1), (e, 3), (e, 4), (e, 5), (e, 6), (e, 7),
        (e, 8), (back_input,), (f, 0), (f, 1), (f, 2), (drain,), (f, 3), (f, 4), (f, 5), (f, 6), (f, 7),
        (f, 8),
    )
    for stage, *at in plan:
        stage(*at)

    drain()
    for copy in stores:
        copy.wait()


def deliver(results):
    steps = 2

    def copy_kernel(*refs):
        for source, target in zip(refs[: len(results)], refs[len(results) :]):
            target[...] = source[...]

    specs = [pl.BlockSpec((TOKENS // steps, D), lambda i: (i, 0))]
    for result in results[1:]:
        specs.append(pl.BlockSpec((8, result.shape[1] // steps), lambda i: (0, i)))
    return pl.pallas_call(
        copy_kernel,
        grid=(steps,),
        out_shape=tuple(jax.ShapeDtypeStruct(x.shape, x.dtype) for x in results),
        in_specs=specs,
        out_specs=tuple(specs),
    )(*results)


def body(
    history,
    qkv_weight,
    out_weight,
    pool_weight,
    head_weight,
    risk_weight,
    time_table,
    case_rows,
    control_rows,
    buckets,
    case_weight,
):
    vmem = pl.BlockSpec(memory_space=pltpu.VMEM)
    smem = pl.BlockSpec(memory_space=pltpu.SMEM)
    hbm = pl.BlockSpec(memory_space=pl.ANY)
    dma = pltpu.SemaphoreType.DMA
    results = pl.pallas_call(
        kernel,
        out_shape=(
            jax.ShapeDtypeStruct((TOKENS, D), F32),
            jax.ShapeDtypeStruct((8, 3 * D), F32),
            jax.ShapeDtypeStruct((8, D), F32),
            jax.ShapeDtypeStruct((8, D), F32),
            jax.ShapeDtypeStruct((8, D), F32),
        ),
        in_specs=[hbm] * 6 + [vmem] * 2 + [smem] * 3,
        out_specs=(hbm,) + (vmem,) * 4,
        scratch_shapes=[
            pltpu.VMEM((TOKENS, D), BF16),
            pltpu.VMEM((D, 3 * D), BF16),
            pltpu.VMEM((D, D), BF16),
            pltpu.VMEM((D, D), BF16),
            pltpu.VMEM((D, D), BF16),
            pltpu.VMEM((NB, D), F32),
            pltpu.VMEM((TOKENS, D), BF16),
            pltpu.VMEM((TOKENS, 1), F32),
            pltpu.VMEM((TOKENS, 3 * D), BF16),
            pltpu.VMEM((R_DEV, PAIRS, 2 * S, S), BF16),
            pltpu.VMEM((TOKENS, D), BF16),
            pltpu.VMEM((TOKENS, D), BF16),
            pltpu.VMEM((TOKENS, D), F32),
            pltpu.VMEM((16, D), F32),
            pltpu.VMEM((MEMBERS, D), BF16),
            pltpu.VMEM((MEMBERS, D), F32),
            pltpu.VMEM((MEMBERS, D), BF16),
            pltpu.VMEM((TOKENS, D), F32),
            pltpu.VMEM((TOKENS, 3 * D), BF16),
            pltpu.VMEM((D, TOKENS), BF16),
            pltpu.VMEM((D, TOKENS), BF16),
            pltpu.VMEM((D, TOKENS), BF16),
            pltpu.VMEM((D, MEMBERS), BF16),
            pltpu.VMEM((16, 8, 128), F32),
            pltpu.VMEM((7, 8, 128), F32),
            pltpu.VMEM((8, 128), F32),
            pltpu.VMEM((4, 128), F32),
            pltpu.VMEM((4, 128), F32),
            pltpu.VMEM((15, 4, 128), F32),
            pltpu.VMEM((7, 4, 128), F32),
            dma((8,)),
            dma((3,)),
            dma((7,)),
            dma((7,)),
            dma((15,)),
            dma((15,)),
            dma((15,)),
            dma((15,)),
            dma((7,)),
            dma((7,)),
            dma((COUNT,)),
            dma((COUNT,)),
            dma((COUNT, 6)),
            dma((COUNT, 6)),
            dma((COUNT, 3)),
            dma((COUNT, 3)),
            dma((COUNT, 3)),
            dma((COUNT, 3)),
        ]
        + [
            pltpu.VMEM((*shape, 16, group[2]), BF16)
            for shape in (
                (2, 4, 4, 4),
                (4, 4, 4),
                (6, 2, 4),
                (4, 4),
                (3, 4),
                (4,),
                (3,),
            )
            for group in GROUPS
        ],
        compiler_params=pltpu.CompilerParams(
            collective_id=1, has_side_effects=True, vmem_limit_bytes=62 * 2**20
        ),
    )(
        history.reshape(TOKENS, D),
        qkv_weight,
        out_weight,
        pool_weight,
        head_weight,
        time_table,
        risk_weight[None],
        control_rows,
        case_rows,
        buckets,
        case_weight,
    )
    grad_input, *shares = deliver(results)
    return (grad_input.reshape(R_DEV, S, D), *shares)


def solution(mesh):
    in_specs = (
        P(("rows", "cols"), None, None),
        P(),
        P(),
        P(),
        P(),
        P(),
        P(),
        P(("rows", "cols")),
        P(("rows", "cols"), None),
        P(("rows", "cols")),
        P(("rows", "cols")),
    )
    out_specs = (
        P(("rows", "cols"), None, None),
        P(("rows", "cols"), None),
        P(("rows", "cols"), None),
        P(("rows", "cols"), None),
        P(("rows", "cols"), None),
    )
    return jax.shard_map(body, mesh=mesh, in_specs=in_specs, out_specs=out_specs, check_vma=False)
```

```python
import math

import jax
import jax.numpy as jnp
from jax import lax
from jax.experimental import pallas as pl
from jax.experimental.pallas import tpu as pltpu
from jax.sharding import PartitionSpec as P

D = 1024
HD = 64
HEADS = 16
S = 128
K = 32
CAP = 4
NB = 128
R_DEV = 3
C_DEV = 3
TOKENS = R_DEV * S
DEVICES = 128
SLOTS = CAP * DEVICES
MEMBERS = SLOTS + 16
PAIRS = HEADS // 2

MESH = pl.DeviceIdType.MESH
F32 = jnp.float32
BF16 = jnp.bfloat16

GROUPS = (
    (("head", 0), ("head", 512), 512, "zyx"),
    (("pool", 0), ("pool", 512), 512, "yxz"),
    (("out", 0), ("out", 512), 512, "xzy"),
    (("qkv", 0), ("qkv", D), 256, "zyx"),
    (("qkv", 256), ("qkv", D + 256), 256, "yxz"),
    (("qkv", 2 * D), ("qkv", 2 * D + 256), 256, "xzy"),
    (("qkv", 512), ("qkv", D + 512), 256, "zyx"),
    (("qkv", 768), ("qkv", D + 768), 256, "yxz"),
    (("qkv", 2 * D + 512), ("qkv", 2 * D + 768), 256, "xzy"),
)
COUNT = len(GROUPS)


def device_at(place):
    return (place["z"] * 4 + place["y"], place["x"] * 2 + place["core"])


def moved(place, axis, step):
    return {**place, axis: lax.rem(place[axis] + step, 4)}


def remote(source, target, send_sem, recv_sem, device):
    return pltpu.make_async_remote_copy(
        src_ref=source,
        dst_ref=target,
        send_sem=send_sem,
        recv_sem=recv_sem,
        device_id=device,
        device_id_type=MESH,
    )


def added(*parts):
    total = parts[0].astype(F32)
    for part in parts[1:]:
        total = total + part.astype(F32)
    return total


def iota(shape, dim):
    return lax.broadcasted_iota(jnp.int32, shape, dim)


def dot(a, b, contract_a=1, contract_b=0):
    return lax.dot_general(
        a, b, (((contract_a,), (contract_b,)), ((), ())), preferred_element_type=F32
    )


def block(i, size):
    return pl.ds(pl.multiple_of(i * size, size), size)


def loop(count, step, unroll=1):
    def run(i, carry):
        step(i)
        return carry

    lax.fori_loop(0, count, run, 0, unroll=unroll)


def find_slots(facts, own, me):
    lane = iota((DEVICES, 128), 1)
    local = facts - (R_DEV * me).astype(F32)
    hit = (lane < C_DEV * K) & (local >= 0.0) & (local < float(R_DEV))
    hits = jnp.where(hit, 1.0, 0.0)
    before = jnp.where(iota((128, 128), 0) < iota((128, 128), 1), 1.0, 0.0).astype(BF16)
    order = dot(hits.astype(BF16), before)
    case_of = jnp.where(lane < K, 0.0, jnp.where(lane < 2 * K, 1.0, 2.0))
    columns = [[], [], [], [], []]
    for j in range(CAP):
        chosen = jnp.where(order == float(j), hits, 0.0)
        row = jnp.sum(chosen * local, axis=1, keepdims=True)
        case = jnp.sum(chosen * case_of, axis=1, keepdims=True)
        taken = jnp.sum(chosen, axis=1, keepdims=True)
        bucket = jnp.zeros_like(row)
        weight = jnp.zeros_like(row)
        for c in range(C_DEV):
            is_c = case == float(c)
            bucket = jnp.where(is_c, facts[:, 96 + c : 97 + c], bucket)
            weight = jnp.where(is_c, facts[:, 99 + c : 100 + c], weight)
        for column, values in zip(columns, (row, case, bucket, weight, taken)):
            column.append(values)
    own_case = iota((16, 1), 0).astype(F32)
    for column, values in zip(
        columns, (own[:, 0:1], own_case, own[:, 1:2], own[:, 2:3], own[:, 3:4])
    ):
        column.append(values)
    return [jnp.concatenate(column, axis=0) for column in columns]


def partial_sums(raised, case, taken, me):
    raised = jnp.where(taken > 0.0, raised, 0.0)
    lane = iota((DEVICES, 128), 1)
    mine = iota((DEVICES, 128), 0) == me
    sums = jnp.zeros((DEVICES, 128), F32)
    for c in range(C_DEV):
        share = jnp.zeros((DEVICES, 1), F32)
        for j in range(CAP):
            at = slice(j * DEVICES, (j + 1) * DEVICES)
            share = share + jnp.where(case[at] == float(c), raised[at], 0.0)
        share = share + jnp.where(mine, raised[SLOTS + c : SLOTS + c + 1], 0.0)
        sums = jnp.where(lane == c, share, sums)
    return sums.T[0:4]


def risk_grads(sums, case, weight, taken, raised, me):
    denominators = jnp.concatenate([sums, jnp.ones((124, 128), F32)], axis=0).T
    wide = jnp.concatenate([sums, jnp.ones((12, 128), F32)], axis=0)
    own = jnp.sum(jnp.where(iota((16, 128), 1) == me, wide, 0.0), axis=1, keepdims=True)
    below = []
    for j in range(CAP):
        of = case[j * DEVICES : (j + 1) * DEVICES]
        below.append(
            jnp.where(
                of == 0.0,
                denominators[:, 0:1],
                jnp.where(of == 1.0, denominators[:, 1:2], denominators[:, 2:3]),
            )
        )
    below = jnp.concatenate(below + [own], axis=0)
    is_case = jnp.where(iota((MEMBERS, 1), 0) >= SLOTS, 1.0, 0.0)
    return jnp.where(taken > 0.0, weight * (raised / below - is_case), 0.0)


def kernel(
    history_in,
    qkv_in,
    out_in,
    pool_in,
    head_in,
    table_in,
    risk_ref,
    control_ref,
    case_rows,
    buckets,
    case_weight,
    grad_input_out,
    qkv_out,
    out_out,
    pool_out,
    head_out,
    history,
    qkv_weight,
    out_weight,
    pool_weight,
    head_weight,
    table,
    normed,
    inverse,
    packed,
    attention,
    mixture,
    residual_low,
    slope,
    pooled,
    hidden,
    head_slope,
    grad_preact,
    grad_residual,
    grad_packed,
    normed_t,
    mixture_t,
    residual_t,
    hidden_t,
    facts,
    facts_in,
    facts_mine,
    sums_own,
    sums_middle,
    sums_row,
    sums_col,
    load_sem,
    store_sem,
    fact_col_send,
    fact_col_recv,
    fact_row_send,
    fact_row_recv,
    sum_row_send,
    sum_row_recv,
    sum_col_send,
    sum_col_recv,
    swap_send,
    swap_recv,
    first_send,
    first_recv,
    second_send,
    second_recv,
    third_send,
    third_recv,
    *buffers,
):
    part, swap, first, second_sum, second, third_sum, third = (
        buffers[i * COUNT : (i + 1) * COUNT] for i in range(7)
    )
    grad_pre, grad_residual_low, grad_mixture = residual_low, normed, mixture
    row = lax.axis_index("rows")
    col = lax.axis_index("cols")
    here = {"z": lax.div(row, 4), "y": lax.rem(row, 4), "x": lax.div(col, 2), "core": lax.rem(col, 2)}
    core = here["core"]
    twin = device_at({**here, "core": 1 - core})
    me = row * 8 + col
    row_peers = [(lax.rem(row + step, 16), col) for step in range(1, 16)]
    col_peers = [(row, lax.rem(col + step, 8)) for step in range(1, 8)]
    sends = []

    def send(copy):
        copy.start()
        sends.append(copy)

    def arrived(target, sem):
        remote(target, target, sem, sem, twin).wait_recv()

    loads = [
        pltpu.make_async_copy(source, target, load_sem.at[i])
        for i, (source, target) in enumerate(
            (
                (history_in, history),
                (qkv_in.at[:, 0:D], qkv_weight.at[:, 0:D]),
                (qkv_in.at[:, D : 2 * D], qkv_weight.at[:, D : 2 * D]),
                (qkv_in.at[:, 2 * D : 3 * D], qkv_weight.at[:, 2 * D : 3 * D]),
                (out_in, out_weight),
                (pool_in, pool_weight),
                (head_in, head_weight),
                (table_in, table),
            )
        )
    ]
    for copy in loads:
        copy.start()
    barrier = pltpu.get_barrier_semaphore()
    for peer in row_peers + col_peers:
        pl.semaphore_signal(barrier, inc=1, device_id=peer, device_id_type=MESH)
    lane = iota((1, 128), 1)
    controls = control_ref[...].astype(F32)
    mine = jnp.concatenate(
        [controls[c : c + 1] for c in range(C_DEV)] + [jnp.zeros((1, 128 - C_DEV * K), F32)], axis=1
    )
    wide_lane, wide_row = iota((16, 128), 1), iota((16, 128), 0)
    own = jnp.where((wide_lane == 3) & (wide_row < C_DEV), 1.0, 0.0)
    for c in range(C_DEV):
        bucket, weight = buckets[c].astype(F32), case_weight[c]
        mine = jnp.where(lane == 96 + c, bucket, mine)
        mine = jnp.where(lane == 99 + c, weight, mine)
        for place, value in enumerate((case_rows[c].astype(F32), bucket, weight)):
            own = jnp.where((wide_lane == place) & (wide_row == c), value, own)
    facts_mine[...] = jnp.broadcast_to(mine, (8, 128))

    loads[0].wait()

    def normalise(r):
        rows = block(r, S)
        x = history[rows, :].astype(F32)
        inv = lax.rsqrt(jnp.mean(x * x, axis=1, keepdims=True) + 1e-05)
        inverse[rows, :] = inv
        normed[rows, :] = (x * inv).astype(BF16)

    loop(R_DEV, normalise, R_DEV)
    pl.semaphore_wait(barrier, len(row_peers) + len(col_peers))
    for i, peer in enumerate(col_peers):
        send(
            remote(facts_mine, facts_in.at[i], fact_col_send.at[i], fact_col_recv.at[i], peer)
        )
    for n in range(3):
        loads[1 + n].wait()
        cols = slice(n * D, (n + 1) * D)
        packed[:, cols] = dot(normed[...], qkv_weight[:, cols]).astype(BF16)

    sub = iota((8, 128), 0)
    tile = jnp.where(sub == col, facts_mine[...], 0.0)
    for i in range(7):
        arrived(facts_in.at[i], fact_col_recv.at[i])
        tile = jnp.where(sub == lax.rem(col + 7 - i, 8), facts_in[i], tile)
    facts[row] = tile
    for i, peer in enumerate(row_peers):
        send(
            remote(facts.at[row], facts.at[row], fact_row_send.at[i], fact_row_recv.at[i], peer)
        )

    for copy in loads[4:]:
        copy.wait()
    low_half = iota((S, 128), 1) < HD

    def halves(values):
        zero = jnp.zeros_like(values)
        return jnp.concatenate(
            [jnp.where(low_half, values, zero), jnp.where(low_half, zero, values)], axis=0
        )

    def joined(values):
        return jnp.where(low_half, values[:S], values[S:])

    def attend(r):
        rows = block(r, S)
        for p in range(PAIRS):
            query = packed[rows, p * 128 : p * 128 + 128]
            key = packed[rows, D + p * 128 : D + p * 128 + 128]
            value = packed[rows, 2 * D + p * 128 : 2 * D + p * 128 + 128]
            raised = jnp.exp(dot(halves(key), query, 1, 1) * (1.0 / math.sqrt(HD)))
            low = jnp.concatenate(
                [
                    raised[:S] * (1.0 / jnp.sum(raised[:S], axis=0, keepdims=True)),
                    raised[S:] * (1.0 / jnp.sum(raised[S:], axis=0, keepdims=True)),
                ],
                axis=0,
            ).astype(BF16)
            attention[r, p] = low
            mixture[rows, p * 128 : p * 128 + 128] = dot(low, halves(value), 0, 0).astype(BF16)

    loop(R_DEV, attend, R_DEV)

    def add_residual(n):
        cols = block(n, 512)
        residual = history[:, cols].astype(F32) + dot(mixture[...], out_weight[:, cols])
        residual_low[:, cols] = residual.astype(BF16)

    loop(2, add_residual, 2)
    sub16 = iota((16, 512), 0)

    def pool(n):
        cols = block(n, 512)
        active = jnp.tanh(dot(residual_low[...], pool_weight[:, cols]))
        slope[:, cols] = (1.0 - active * active) * (1.0 / math.sqrt(S))
        rows = jnp.zeros((16, 512), F32)
        for r in range(R_DEV):
            total = jnp.sum(active[r * S : (r + 1) * S], axis=0, keepdims=True)
            rows = jnp.where(sub16 == r, total * (1.0 / math.sqrt(S)), rows)
        pooled[:, cols] = rows.astype(BF16).astype(F32)

    loop(2, pool, 2)

    for i in range(15):
        source = lax.rem(row + 15 - i, 16)
        arrived(facts.at[source], fact_row_recv.at[i])
    at_row, case, bucket, weight, taken = find_slots(facts[...].reshape(DEVICES, 128), own, me)
    onehot = jnp.where(iota((MEMBERS, NB), 1).astype(F32) == bucket, 1.0, 0.0).astype(BF16)
    onehots = jnp.concatenate([onehot] * 3, axis=1)

    def embed(n):
        cols = block(n, 512)
        times = table[:, cols]
        high = times.astype(BF16)
        middle = (times - high.astype(F32)).astype(BF16)
        low = (times - high.astype(F32) - middle.astype(F32)).astype(BF16)
        rows = pooled[:, cols]
        picked = jnp.where(at_row == 0.0, rows[0:1], jnp.where(at_row == 1.0, rows[1:2], rows[2:3]))
        hidden[:, cols] = (
            picked + dot(onehots, jnp.concatenate([high, middle, low], axis=0))
        ).astype(BF16)

    loop(2, embed, 2)

    def score(n, total):
        cols = block(n, 512)
        preact = dot(hidden[...], head_weight[:, cols])
        gated = jax.nn.sigmoid(preact)
        risk = risk_ref[:, cols]
        head_slope[:, cols] = risk * gated * (1.0 + preact * (1.0 - gated))
        return total + jnp.sum(preact * gated * risk, axis=1, keepdims=True)

    raised = jnp.exp(lax.fori_loop(0, 2, score, jnp.zeros((MEMBERS, 1), F32), unroll=2))

    sums = partial_sums(raised, case, taken, me)
    sums_own[...] = sums
    for i, peer in enumerate(row_peers):
        send(remote(sums_own, sums_row.at[i], sum_row_send.at[i], sum_row_recv.at[i], peer))
    normed_t[...] = normed[...].T
    mixture_t[...] = mixture[...].T
    for i in range(15):
        arrived(sums_row.at[i], sum_row_recv.at[i])
        sums = sums + sums_row[i]
    sums_middle[...] = sums
    for i, peer in enumerate(col_peers):
        send(remote(sums_middle, sums_col.at[i], sum_col_send.at[i], sum_col_recv.at[i], peer))
    residual_t[...] = residual_low[...].T
    hidden_t[...] = hidden[...].T
    for i in range(7):
        arrived(sums_col.at[i], sum_col_recv.at[i])
        sums = sums + sums_col[i]

    grad_risk = risk_grads(sums, case, weight, taken, raised, me)
    row_of = jnp.where(
        (iota((MEMBERS, 128), 1).astype(F32) == at_row) & (taken > 0.0), 1.0, 0.0
    ).astype(BF16)

    def score_grad(n):
        cols = block(n, 512)
        grad = (grad_risk * head_slope[:, cols]).astype(BF16)
        grad_preact[:, cols] = grad
        pooled[:, cols] = dot(row_of, grad, 0, 0)[0:16]

    loop(2, score_grad, 2)
    sides = {
        "head": (hidden_t, 1, grad_preact, head_out),
        "pool": (residual_t, 1, grad_pre, pool_out),
        "out": (mixture_t, 1, grad_residual_low, out_out),
        "qkv": (normed_t, 1, grad_packed, qkv_out),
    }

    def produce(g):
        width, order = GROUPS[g][2:]
        results = []
        for name, col0 in GROUPS[g][:2]:
            lhs, contract, rhs, _ = sides[name]
            grad = dot(lhs[...], rhs[:, col0 : col0 + width], contract, 0)
            results.append(grad.reshape(4, 4, 4, 2, 8, width))
        for c in range(2):
            for z in range(4):
                for y in range(4):
                    values = jnp.concatenate(
                        [result[z, y, :, c] for result in results], axis=1
                    ).astype(BF16)
                    if order == "zyx":
                        part[g][c, z, y] = values
                    elif order == "yxz":
                        part[g][c, y, :, z] = values
                    else:
                        part[g][c, :, z, y] = values
        send(remote(part[g].at[1 - core], swap[g], swap_send.at[g], swap_recv.at[g], twin))

    def ring(g):
        at = here[GROUPS[g][3][0]]
        return at, lax.rem(at + 1, 4), lax.rem(at + 2, 4), lax.rem(at + 3, 4)

    def send_first(g, slot, digit, half, step):
        send(
            remote(
                part[g].at[core, digit, pl.ds(half, 2)],
                first[g].at[slot],
                first_send.at[g, slot],
                first_recv.at[g, slot],
                device_at(moved(here, GROUPS[g][3][0], step)),
            )
        )

    def first_spread(g):
        at, right, far, left = ring(g)
        arrived(swap[g], swap_recv.at[g])
        for b in range(4):
            part[g][core, far, b] = added(part[g][core, far, b], swap[g][far, b]).astype(BF16)
        send_first(g, 0, far, 0, 1)
        send_first(g, 1, far, 2, 3)
        for b in range(2):
            part[g][core, right, 2 + b] = added(
                part[g][core, right, 2 + b], swap[g][right, 2 + b]
            ).astype(BF16)
            part[g][core, left, b] = added(part[g][core, left, b], swap[g][left, b]).astype(BF16)
        send_first(g, 2, right, 2, 1)
        send_first(g, 3, left, 0, 3)

    def first_relay(g):
        at, right, far, left = ring(g)
        for slot, came, digit, half, step in ((4, 0, right, 0, 1), (5, 1, left, 2, 3)):
            arrived(first[g].at[came], first_recv.at[g, came])
            for k in range(2):
                b = half + k
                part[g][core, digit, b] = added(
                    part[g][core, digit, b], swap[g][digit, b], first[g][came, k]
                ).astype(BF16)
            send_first(g, slot, digit, half, step)

    def second_spread(g):
        at = ring(g)[0]
        for slot in (2, 3, 4, 5):
            arrived(first[g].at[slot], first_recv.at[g, slot])
        for b in range(4):
            one, other = (3, 4) if b < 2 else (2, 5)
            second_sum[g][b] = added(
                part[g][core, at, b], swap[g][at, b], first[g][one, b % 2], first[g][other, b % 2]
            ).astype(BF16)
        direct(GROUPS[g][3][1], second_sum[g], second[g], second_send.at[g], second_recv.at[g])

    def direct(axis, source, landing, send_sems, recv_sems):
        for step in (2, 1, 3):
            send(
                remote(
                    source.at[lax.rem(here[axis] + step, 4)],
                    landing.at[step - 1],
                    send_sems.at[step - 1],
                    recv_sems.at[step - 1],
                    device_at(moved(here, axis, step)),
                )
            )

    def third_spread(g):
        at = here[GROUPS[g][3][1]]
        for slot in range(3):
            arrived(second[g].at[slot], second_recv.at[g, slot])
        third_sum[g][...] = added(second_sum[g][at], second[g][0], second[g][1], second[g][2]).astype(
            BF16
        )
        direct(GROUPS[g][3][2], third_sum[g], third[g], third_send.at[g], third_recv.at[g])

    def finish(g):
        width, order = GROUPS[g][2:]
        for slot in range(3):
            arrived(third[g].at[slot], third_recv.at[g, slot])
        total = added(third_sum[g][here[order[2]]], third[g][0], third[g][1], third[g][2])
        for t, (name, col0) in enumerate(GROUPS[g][:2]):
            sides[name][3][:, col0 : col0 + width] = total[8 * t : 8 * t + 8]

    def back_pooled():
        by_row = pooled[...]
        high = by_row.astype(BF16)
        low = (by_row - high.astype(F32)).astype(BF16)
        by_row = jnp.concatenate([high, low], axis=0)

        def pool_grad(n):
            both = dot(by_row, head_weight[block(n, 512), :], 1, 1)
            grad = both[0:16] + both[16:32]
            cols = block(n, 512)
            for r in range(R_DEV):
                rows = slice(r * S, (r + 1) * S)
                grad_pre[rows, cols] = (grad[r : r + 1] * slope[rows, cols]).astype(BF16)

        loop(2, pool_grad, 2)

    def back_residual():
        def step(n):
            cols = block(n, 512)
            grad = dot(grad_pre[...], pool_weight[cols, :], 1, 1)
            grad_residual[:, cols] = grad
            grad_residual_low[:, cols] = grad.astype(BF16)

        loop(2, step, 2)

    def back_mixture():
        def step(n):
            cols = block(n, 512)
            grad_mixture[:, cols] = dot(grad_residual_low[...], out_weight[cols, :], 1, 1).astype(BF16)

        loop(2, step, 2)

    def back_attend_one(r, p):
        rows = slice(r * S, (r + 1) * S)
        query_at, key_at, value_at = (slice(i * D + p * 128, i * D + p * 128 + 128) for i in range(3))
        query, key, value = packed[rows, query_at], packed[rows, key_at], packed[rows, value_at]
        grad = grad_mixture[rows, query_at]
        low = attention[r, p]
        weights = low.astype(F32)
        grad_attention = dot(halves(value), grad, 1, 1)
        product = weights * grad_attention
        scale = 1.0 / math.sqrt(HD)
        grad_logits = jnp.concatenate(
            [
                weights[at]
                * (grad_attention[at] - jnp.sum(product[at], axis=0, keepdims=True))
                * scale
                for at in (slice(0, S), slice(S, 2 * S))
            ],
            axis=0,
        ).astype(BF16)
        grad_packed[rows, query_at] = dot(grad_logits, halves(key), 0, 0).astype(BF16)
        grad_packed[rows, key_at] = joined(dot(grad_logits, query)).astype(BF16)
        grad_packed[rows, value_at] = joined(dot(low, grad)).astype(BF16)

    def back_attend(first_pair, pairs):
        for r in range(R_DEV):
            for p in range(first_pair, first_pair + pairs):
                back_attend_one(r, p)

    def back_normed(n):
        cols = slice(n * 512, (n + 1) * 512)
        head_slope[0:TOKENS, cols] = dot(grad_packed[...], qkv_weight[cols, :], 1, 1)

    stores = []

    def back_input():
        for r in range(R_DEV):
            rows = slice(r * S, (r + 1) * S)
            grad = head_slope[rows, :]
            x = history[rows, :].astype(F32)
            inv = inverse[rows, :]
            mean = jnp.mean(grad * x, axis=1, keepdims=True)
            head_slope[rows, :] = grad_residual[rows, :] + inv * grad - x * (inv * inv * inv * mean)
            stores.append(
                pltpu.make_async_copy(head_slope.at[rows], grad_input_out.at[rows], store_sem.at[r])
            )
            stores[-1].start()

    a, b, c, d, e, f = produce, first_spread, first_relay, second_spread, third_spread, finish
    def drain():
        while sends:
            sends.pop(0).wait_send()

    plan = (
        (a, 0), (back_pooled,), (a, 1), (back_residual,), (b, 0), (a, 2), (b, 1), (back_mixture,), (b, 2),
        (back_attend, 0, 4), (a, 3), (a, 4), (a, 5), (c, 0), (c, 1), (c, 2), (b, 3), (b, 4), (b, 5),
        (back_attend, 4, 4), (a, 6), (a, 7), (a, 8), (d, 0), (d, 1), (c, 3), (c, 4), (b, 6), (b, 7),
        (b, 8), (c, 5), (d, 2), (e, 0), (e, 1), (c, 6), (c, 7), (c, 8), (back_normed, 0), (d, 3), (d, 4),
        (d, 5), (e, 2), (d, 6), (d, 7), (d, 8), (back_normed, 1), (e, 3), (e, 4), (e, 5), (e, 6), (e, 7),
        (e, 8), (back_input,), (f, 0), (f, 1), (f, 2), (drain,), (f, 3), (f, 4), (f, 5), (f, 6), (f, 7),
        (f, 8),
    )
    for stage, *at in plan:
        stage(*at)

    drain()
    for copy in stores:
        copy.wait()


def deliver(results):
    steps = 2

    def copy_kernel(*refs):
        for source, target in zip(refs[: len(results)], refs[len(results) :]):
            target[...] = source[...]

    specs = [pl.BlockSpec((TOKENS // steps, D), lambda i: (i, 0))]
    for result in results[1:]:
        specs.append(pl.BlockSpec((8, result.shape[1] // steps), lambda i: (0, i)))
    return pl.pallas_call(
        copy_kernel,
        grid=(steps,),
        out_shape=tuple(jax.ShapeDtypeStruct(x.shape, x.dtype) for x in results),
        in_specs=specs,
        out_specs=tuple(specs),
    )(*results)


def body(
    history,
    qkv_weight,
    out_weight,
    pool_weight,
    head_weight,
    risk_weight,
    time_table,
    case_rows,
    control_rows,
    buckets,
    case_weight,
):
    vmem = pl.BlockSpec(memory_space=pltpu.VMEM)
    smem = pl.BlockSpec(memory_space=pltpu.SMEM)
    hbm = pl.BlockSpec(memory_space=pl.ANY)
    dma = pltpu.SemaphoreType.DMA
    results = pl.pallas_call(
        kernel,
        out_shape=(
            jax.ShapeDtypeStruct((TOKENS, D), F32),
            jax.ShapeDtypeStruct((8, 3 * D), F32),
            jax.ShapeDtypeStruct((8, D), F32),
            jax.ShapeDtypeStruct((8, D), F32),
            jax.ShapeDtypeStruct((8, D), F32),
        ),
        in_specs=[hbm] * 6 + [vmem] * 2 + [smem] * 3,
        out_specs=(hbm,) + (vmem,) * 4,
        scratch_shapes=[
            pltpu.VMEM((TOKENS, D), BF16),
            pltpu.VMEM((D, 3 * D), BF16),
            pltpu.VMEM((D, D), BF16),
            pltpu.VMEM((D, D), BF16),
            pltpu.VMEM((D, D), BF16),
            pltpu.VMEM((NB, D), F32),
            pltpu.VMEM((TOKENS, D), BF16),
            pltpu.VMEM((TOKENS, 1), F32),
            pltpu.VMEM((TOKENS, 3 * D), BF16),
            pltpu.VMEM((R_DEV, PAIRS, 2 * S, S), BF16),
            pltpu.VMEM((TOKENS, D), BF16),
            pltpu.VMEM((TOKENS, D), BF16),
            pltpu.VMEM((TOKENS, D), F32),
            pltpu.VMEM((16, D), F32),
            pltpu.VMEM((MEMBERS, D), BF16),
            pltpu.VMEM((MEMBERS, D), F32),
            pltpu.VMEM((MEMBERS, D), BF16),
            pltpu.VMEM((TOKENS, D), F32),
            pltpu.VMEM((TOKENS, 3 * D), BF16),
            pltpu.VMEM((D, TOKENS), BF16),
            pltpu.VMEM((D, TOKENS), BF16),
            pltpu.VMEM((D, TOKENS), BF16),
            pltpu.VMEM((D, MEMBERS), BF16),
            pltpu.VMEM((16, 8, 128), F32),
            pltpu.VMEM((7, 8, 128), F32),
            pltpu.VMEM((8, 128), F32),
            pltpu.VMEM((4, 128), F32),
            pltpu.VMEM((4, 128), F32),
            pltpu.VMEM((15, 4, 128), F32),
            pltpu.VMEM((7, 4, 128), F32),
            dma((8,)),
            dma((3,)),
            dma((7,)),
            dma((7,)),
            dma((15,)),
            dma((15,)),
            dma((15,)),
            dma((15,)),
            dma((7,)),
            dma((7,)),
            dma((COUNT,)),
            dma((COUNT,)),
            dma((COUNT, 6)),
            dma((COUNT, 6)),
            dma((COUNT, 3)),
            dma((COUNT, 3)),
            dma((COUNT, 3)),
            dma((COUNT, 3)),
        ]
        + [
            pltpu.VMEM((*shape, 16, group[2]), BF16)
            for shape in (
                (2, 4, 4, 4),
                (4, 4, 4),
                (6, 2, 4),
                (4, 4),
                (3, 4),
                (4,),
                (3,),
            )
            for group in GROUPS
        ],
        compiler_params=pltpu.CompilerParams(
            collective_id=1, has_side_effects=True, vmem_limit_bytes=62 * 2**20
        ),
    )(
        history.reshape(TOKENS, D),
        qkv_weight,
        out_weight,
        pool_weight,
        head_weight,
        time_table,
        risk_weight[None],
        control_rows,
        case_rows,
        buckets,
        case_weight,
    )
    grad_input, *shares = deliver(results)
    return (grad_input.reshape(R_DEV, S, D), *shares)


def solution(mesh):
    in_specs = (
        P(("rows", "cols"), None, None),
        P(),
        P(),
        P(),
        P(),
        P(),
        P(),
        P(("rows", "cols")),
        P(("rows", "cols"), None),
        P(("rows", "cols")),
        P(("rows", "cols")),
    )
    out_specs = (
        P(("rows", "cols"), None, None),
        P(("rows", "cols"), None),
        P(("rows", "cols"), None),
        P(("rows", "cols"), None),
        P(("rows", "cols"), None),
    )
    return jax.shard_map(body, mesh=mesh, in_specs=in_specs, out_specs=out_specs, check_vma=False)
```
